32 devices in a mesh: design: 2 (over x), gx: 4 (over y, core), gy: 4 (over z).
Axes of the slice: x: 2, y: 2, z: 4, core: 2. Of those that a mesh axis runs over, the one named last changes fastest.
Arguments:
- e_field: float32 [6, 16, 64, 512], P('design', None, 'gx', 'gy'), parts along dimension 0, may hold values from -6 to 6
- h_field: float32 [6, 16, 64, 512], P('design', None, 'gx', 'gy'), parts along dimension 0, may hold values from -6 to 6
- inverse_permittivity: float32 [32, 64, 512], P('design', 'gx', 'gy'), parts along dimension 0, may hold values from 0.0833 to 1
- monitor_layer: int32 [128, 512], P(('design', 'gx'), 'gy'), parts along dimension 0, may hold values from 0 to 15
- source_layer: int32 [128, 512], P(('design', 'gx'), 'gy'), parts along dimension 0, may hold values from 0 to 15
- residual_far: float32 [4, 2, 2, 256, 256], P('design', None, None, 'gx', 'gy'), parts along dimension 0, may hold values from -6 to 6
Outputs:
- e_forward: float32 [6, 16, 64, 512], P('design', None, 'gx', 'gy'), parts along dimension 0
- far_field: float32 [4, 2, 2, 256, 256], P('design', None, None, 'gx', 'gy'), parts along dimension 0
- e_adjoint: float32 [6, 16, 64, 512], P('design', None, 'gx', 'gy'), parts along dimension 0
The draws below stay inside these ranges and needn't reach their ends.
There are 2 independent parts, one for each index of `design`. The reference program is written for one: setup_inputs(seed, part) draws one part's arguments, and reference() takes and returns one part's arrays. A program takes and returns all parts, laid end to end along the dimension named above; each array names one. Nothing has to cross between parts.
All inputs are finite; a program needn't handle non-finite values.
Results may differ from the reference program's by a relative error of at most 0.0001.
Values sent between devices are 32-bit elements; how exact they have to be, the bound alone decides.
A program may use at most 64 MiB of HBM per device.

```python
import math
import jax
import jax.numpy as jnp
from jax import lax

NZ = 16
DIRS = 256
NX = 64
NY = 512


def set_ends(drawn, own_key, smallest, largest):
    extent = drawn.shape
    spot = [jax.random.randint(jax.random.fold_in(own_key, axis), (), 0, extent[axis]) for axis in range(len(extent))]
    drawn = drawn.at[tuple(spot)].set(smallest)
    longest = extent.index(max(extent))
    spot[longest] = (spot[longest] + 1) % extent[longest]
    return drawn.at[tuple(spot)].set(largest)


def block_levels(key, dims, shards, smallest, largest):
    loudness, own = 1.0, jax.random.fold_in(key, 6)
    for dim, parts in shards:
        steps = jnp.exp(jax.random.uniform(jax.random.fold_in(own, dim), (parts,), jnp.float32, smallest / len(shards), largest / len(shards)))
        loudness = loudness * jnp.repeat(steps, dims[dim] // parts).reshape([-1 if axis == dim else 1 for axis in range(len(dims))])
    return loudness


def centred(key, dims, width, limit, split=(), kind=jnp.bfloat16):
    gain = block_levels(key, dims, split, -0.22, 0.18) if split else 1.0
    result = jax.random.normal(key, dims, jnp.float32) * width * gain
    return jnp.minimum(jnp.maximum(result, -limit), limit).astype(kind)


def setup_inputs(seed: int = 0, part: int = 0) -> dict:
    keys = jax.random.split(jax.random.key(seed), 7)
    part_keys = jax.random.split(jax.random.fold_in(keys[6], part), 7)
    e_field = centred(part_keys[0], (3, NZ, NX, NY), 1.0, 6.0, ((2, 4), (3, 4)), jnp.float32)
    h_field = centred(part_keys[1], (3, NZ, NX, NY), 1.0, 6.0, ((2, 4), (3, 4)), jnp.float32)
    inverse_permittivity = jnp.clip(jnp.exp(math.log(1.0) - 2.4853067 * jax.random.uniform(part_keys[2], (NZ, NX, NY), jnp.float32) ** block_levels(part_keys[2], (NZ, NX, NY), ((1, 4), (2, 4)), -0.2, 0.2)), 0.0833, 1.0)
    monitor_layer = set_ends(jax.random.randint(part_keys[3], (NX, NY), 0, NZ), jax.random.fold_in(part_keys[3], 1), 0, NZ - 1).astype(jnp.int32)
    source_layer = set_ends(jax.random.randint(part_keys[4], (NX, NY), 0, NZ), jax.random.fold_in(part_keys[4], 1), 0, NZ - 1).astype(jnp.int32)
    residual_far = centred(part_keys[5], (2, 2, 2, DIRS, DIRS), 1.0, 6.0, ((3, 4), (4, 4)), jnp.float32)
    return dict(e_field=e_field, h_field=h_field, inverse_permittivity=inverse_permittivity, monitor_layer=monitor_layer, source_layer=source_layer, residual_far=residual_far)


courant = 0.5
omegas = (0.7, 1.3)
factors = (3, 5)
highest = lax.Precision.HIGHEST

def contract(form, left, right):
    return jnp.einsum(form, left, right, precision=highest)

def ahead(field, along):
    count = field.shape[along]
    widths = [(0, 0)] * field.ndim
    widths[along] = (0, 1)
    return jnp.pad(lax.slice_in_dim(field, 1, count, axis=along), widths)

def behind(field, along):
    count = field.shape[along]
    widths = [(0, 0)] * field.ndim
    widths[along] = (1, 0)
    return jnp.pad(lax.slice_in_dim(field, 0, count - 1, axis=along), widths)

def phase_pair(rows, cols, length):
    cosines = []
    sines = []
    for factor in factors:
        index = jnp.mod((rows[:, None] - DIRS // 2) * cols[None, :] * factor, 4 * length)
        angle = index.astype(jnp.float32) * (2.0 * math.pi / (4 * length))
        cosines.append(jnp.cos(angle))
        sines.append(jnp.sin(angle))
    return (jnp.stack(cosines), jnp.stack(sines))

def step_magnetic(elec, magn):
    curl_x = ahead(elec[2], 2) - elec[2] - (ahead(elec[1], 0) - elec[1])
    curl_y = ahead(elec[0], 0) - elec[0] - (ahead(elec[2], 1) - elec[2])
    curl_z = ahead(elec[1], 1) - elec[1] - (ahead(elec[0], 2) - elec[0])
    return magn - courant * jnp.stack([curl_x, curl_y, curl_z])

def step_electric(elec, magn, inverse, current):
    curl_x = magn[2] - behind(magn[2], 2) - (magn[1] - behind(magn[1], 0))
    curl_y = magn[0] - behind(magn[0], 0) - (magn[2] - behind(magn[2], 1))
    curl_z = magn[1] - behind(magn[1], 1) - (magn[0] - behind(magn[0], 2))
    if current is not None:
        curl_x = curl_x - current[0]
        curl_y = curl_y - current[1]
    return elec + courant * inverse[None] * jnp.stack([curl_x, curl_y, curl_z])

def reference(e_field, h_field, inverse_permittivity, monitor_layer, source_layer, residual_far):
    elec = e_field
    magn = h_field
    watch = (jnp.arange(NZ, dtype=jnp.int32)[:, None, None] == monitor_layer[None]).astype(jnp.float32)
    planes = []
    for moment in range(2):
        magn = step_magnetic(elec, magn)
        elec = step_electric(elec, magn, inverse_permittivity, None)
        planes.append(lax.optimization_barrier(jnp.sum(elec[:2] * watch[None], axis=1)))
    e_forward = elec
    spec_real = jnp.stack([math.cos(omega) * planes[0] + math.cos(2 * omega) * planes[1] for omega in omegas])
    spec_imag = jnp.stack([-(math.sin(omega) * planes[0] + math.sin(2 * omega) * planes[1]) for omega in omegas])
    directions = jnp.arange(DIRS, dtype=jnp.int32)
    cos_x, sin_x = phase_pair(directions, jnp.arange(NX, dtype=jnp.int32), NX)
    cos_y, sin_y = phase_pair(directions, jnp.arange(NY, dtype=jnp.int32), NY)
    q_real = contract('fax,fcxy->fcay', cos_x, spec_real) + contract('fax,fcxy->fcay', sin_x, spec_imag)
    q_imag = contract('fax,fcxy->fcay', cos_x, spec_imag) - contract('fax,fcxy->fcay', sin_x, spec_real)
    a_real = contract('fcay,fby->fcab', q_real, cos_y) + contract('fcay,fby->fcab', q_imag, sin_y)
    a_imag = contract('fcay,fby->fcab', q_imag, cos_y) - contract('fcay,fby->fcab', q_real, sin_y)
    far_field = jnp.stack([a_real, a_imag], axis=2) * (1.0 / math.sqrt(NX * NY))
    res_real = residual_far[:, :, 0]
    res_imag = residual_far[:, :, 1]
    u_real = contract('fcab,fby->fcay', res_real, cos_y) - contract('fcab,fby->fcay', res_imag, sin_y)
    u_imag = contract('fcab,fby->fcay', res_real, sin_y) + contract('fcab,fby->fcay', res_imag, cos_y)
    s_real = (contract('fax,fcay->fcxy', cos_x, u_real) - contract('fax,fcay->fcxy', sin_x, u_imag)) / DIRS
    s_imag = (contract('fax,fcay->fcxy', cos_x, u_imag) + contract('fax,fcay->fcxy', sin_x, u_real)) / DIRS
    layers = (jnp.arange(NZ, dtype=jnp.int32)[:, None, None] == source_layer[None]).astype(jnp.float32)
    elec = jnp.zeros_like(e_field)
    magn = jnp.zeros_like(h_field)
    for moment in range(2):
        tick = moment + 1
        drive = s_real[0] * math.cos(omegas[0] * tick) - s_imag[0] * math.sin(omegas[0] * tick)
        drive = drive + s_real[1] * math.cos(omegas[1] * tick) - s_imag[1] * math.sin(omegas[1] * tick)
        current = layers[None] * drive[:, None]
        magn = step_magnetic(elec, magn)
        elec = step_electric(elec, magn, inverse_permittivity, current)
    return (e_forward, far_field, elec)
```

```python
import functools
import math

import jax
import jax.numpy as jnp
import ml_dtypes
import numpy as np
from jax import lax
from jax.experimental import pallas as pl
from jax.experimental.pallas import tpu as pltpu
from jax.sharding import PartitionSpec as P

courant = 0.5
omegas = (0.7, 1.3)
factors = (3, 5)
MESH = pl.DeviceIdType.MESH
ticks = (1, 2)


def halves(table):
    high = table.astype(ml_dtypes.bfloat16)
    low = (table - high.astype(np.float64)).astype(ml_dtypes.bfloat16)
    return np.stack([high, low], axis=-3)


def angles(dirs, length):
    rows = np.arange(dirs)[:, None] - dirs // 2
    cols = np.arange(length)[None, :]
    return np.stack(
        [np.mod(rows * cols * factor, 4 * length) * (2.0 * np.pi / (4 * length)) for factor in factors]
    )


def tables(gx, gy, na, nb, nx, ny):
    theta = angles(gx * na, gx * nx)
    phi = angles(gy * nb, gy * ny)
    freqs = len(factors)
    shifted = np.stack([phi + np.array(omegas)[:, None, None] * t for t in ticks])
    both = np.stack([np.cos(shifted), -np.sin(shifted)], axis=2)
    both = both.reshape(len(ticks), freqs, 2, gy, nb, gy, ny)
    far_y = both.transpose(3, 0, 5, 6, 1, 2, 4).reshape(gy, len(ticks), gy, ny, freqs * 2 * nb)
    back_y = both.transpose(5, 3, 1, 2, 4, 0, 6).reshape(gy, gy, freqs, 2 * nb, len(ticks) * ny)
    back_y = back_y / (gx * na)
    pair = np.stack([np.cos(theta), np.sin(theta)], axis=1).reshape(freqs, 2, gx, na, gx * nx)
    far_x = pair.transpose(2, 0, 1, 3, 4).reshape(gx, freqs, 2 * na, gx * nx)
    far_x = far_x / math.sqrt(gx * nx * gy * ny)
    cos, sin = np.cos(theta), np.sin(theta)
    mix = np.stack([np.stack([cos, -sin]), np.stack([sin, cos])])
    mix = mix.reshape(2, 2, freqs, gx, na, gx, nx)
    back_x = mix.transpose(3, 2, 5, 0, 6, 1, 4).reshape(gx, freqs, gx * 2 * nx, 2 * na)
    return halves(far_y), halves(back_y), halves(far_x), halves(back_x)


def split(value):
    high = value.astype(jnp.bfloat16)
    return high, (value - high.astype(jnp.float32)).astype(jnp.bfloat16)


def mul(left, right):
    return jnp.dot(left, right, preferred_element_type=jnp.float32)


def triple(left, right):
    return mul(left[0], right[0]) + (mul(left[0], right[1]) + mul(left[1], right[0]))


def kernel(
    gx, gy,
    e_in, h_in, k_in, mon_in, src_in, res_in, far_y_in, back_y_in, far_x_in, back_x_in,
    e_out, far_out, adj_out,
    elec, magn, inv, mon, src, res, far_y, back_y, far_x, back_x,
    aelec, amagn, afinal, far,
    row_send, col_send, row_recv, col_recv,
    vsend, vrecv, vall, planes, qall,
    in_sems, out_sems, halo_send, halo_recv, v_send, v_recv, g_send, g_recv, p_send, p_recv, q_send, q_recv,
):
    mx = lax.axis_index("gx")
    my = lax.axis_index("gy")
    _, nz, nx, ny = e_in.shape
    na, nb = res_in.shape[3:]
    freqs = len(factors)

    loads = {}
    for slot, (name, source, target) in enumerate((
        ("res", res_in, res),
        ("back_x", back_x_in.at[mx], back_x),
        ("e", e_in, elec.at[:, pl.ds(0, nz)]),
        ("h", h_in, magn.at[:, pl.ds(1, nz)]),
        ("k", k_in, inv),
        ("mon", mon_in, mon),
        ("src", src_in, src),
        ("back_y", back_y_in.at[my], back_y),
        ("far_y", far_y_in.at[my], far_y),
        ("far_x", far_x_in.at[mx], far_x),
    )):
        loads[name] = pltpu.make_async_copy(source, target, in_sems.at[slot])
        loads[name].start()

    row_recv[...] = jnp.zeros_like(row_recv)
    col_recv[...] = jnp.zeros_like(col_recv)
    blank = jnp.zeros((nx, ny), jnp.float32)
    for part in range(3):
        elec[part, nz] = blank
        magn[part, 0] = blank
        amagn[part, 0] = blank
    for part in range(2):
        aelec[part, nz] = blank

    barrier = pltpu.get_barrier_semaphore()
    for step in range(1, gx):
        pl.semaphore_signal(barrier, inc=1, device_id={"gx": lax.rem(mx + step, gx)}, device_id_type=MESH)
    for step in range(1, gy):
        pl.semaphore_signal(barrier, inc=1, device_id={"gy": lax.rem(my + step, gy)}, device_id_type=MESH)

    lanes = lax.broadcasted_iota(jnp.int32, (nx, ny), 1)
    rows = lax.broadcasted_iota(jnp.int32, (nx, ny), 0)

    def each_z(body, init):
        return lax.fori_loop(0, nz, body, init, unroll=True)

    def ahead_x(value, edge):
        return jnp.where(rows == nx - 1, edge, pltpu.roll(value, nx - 1, axis=0))

    def behind_x(value, edge):
        return jnp.where(rows == 0, edge, pltpu.roll(value, 1, axis=0))

    def ahead_y(value, packed, lane):
        edge = pltpu.roll(packed, lax.rem(2 * ny - 1 - lane, ny), axis=1)
        return jnp.where(lanes == ny - 1, edge, pltpu.roll(value, ny - 1, axis=1))

    def behind_y(value, packed, lane):
        edge = pltpu.roll(packed, lax.rem(2 * ny - lane, ny), axis=1)
        return jnp.where(lanes == 0, edge, pltpu.roll(value, 1, axis=1))

    def pack_first(value, lane, packed):
        return jnp.where(lanes == lane, pltpu.roll(value, lane, axis=1), packed)

    def pack_last(value, lane, packed):
        return jnp.where(lanes == lane, pltpu.roll(value, lane + 1, axis=1), packed)

    def halo(number, direction, count):
        size = gx, gy
        place = mx, my
        out = []
        for which, (axis, send, recv) in enumerate((("gx", row_send, row_recv), ("gy", col_send, col_recv))):
            here, total = place[which], size[which]
            target = lax.rem(here + direction + total, total)
            source_ref = send.at[number, pl.ds(0, count)] if which == 0 else send.at[number]
            target_ref = recv.at[number, pl.ds(0, count)] if which == 0 else recv.at[number]
            copy = pltpu.make_async_remote_copy(
                src_ref=source_ref,
                dst_ref=target_ref,
                send_sem=halo_send.at[number, which],
                recv_sem=halo_recv.at[number, which],
                device_id={axis: target},
                device_id_type=MESH,
            )
            sends = here >= 1 if direction < 0 else here < total - 1
            takes = here < total - 1 if direction < 0 else here >= 1
            out.append((copy, sends, takes))
        return out

    halos = [halo(number, direction, count) for number, (direction, count) in enumerate(
        ((-1, 2), (1, 2), (-1, 2), (1, 2), (-1, 1), (1, 2)))]

    def send_halo(number):
        for copy, sends, _ in halos[number]:
            pl.when(sends)(copy.start)

    def take_halo(number):
        for copy, _, takes in halos[number]:
            pl.when(takes)(copy.wait_recv)

    def end_halo(number):
        for copy, sends, _ in halos[number]:
            pl.when(sends)(copy.wait_send)

    def spread(axis, source, target, send, recv):
        here, total = (mx, gx) if axis == "gx" else (my, gy)
        out = []
        for step in range(1, total):
            other = lax.rem(here + step, total)
            out.append((
                pltpu.make_async_remote_copy(
                    src_ref=source(other), dst_ref=target(here),
                    send_sem=send(other), recv_sem=recv(here),
                    device_id={axis: other}, device_id_type=MESH),
                pltpu.make_async_remote_copy(
                    src_ref=source(other), dst_ref=target(other),
                    send_sem=send(other), recv_sem=recv(other),
                    device_id={axis: other}, device_id_type=MESH),
            ))
        return out

    def start(copies):
        for copy, _ in copies:
            copy.start()

    def arrive(copies):
        for _, copy in copies:
            copy.wait_recv()

    def left(copies):
        for copy, _ in copies:
            copy.wait_send()

    loads["res"].wait()
    loads["back_x"].wait()
    for f in range(freqs):
        block = jnp.concatenate(
            [jnp.concatenate([res[f, c, 0], res[f, c, 1]], axis=0) for c in range(2)], axis=1)
        part = triple((back_x[f, 0], back_x[f, 1]), split(block))
        for other in range(gx):
            vsend[other, f] = part[other * 2 * nx:(other + 1) * 2 * nx]

    loads["e"].wait()

    def pack_start(z, packed):
        row_send[0, 0, pl.ds(z, 1)] = elec[1, z, 0:1]
        row_send[0, 1, pl.ds(z, 1)] = elec[2, z, 0:1]
        packed = pack_first(elec[0, z], z, packed)
        return pack_first(elec[2, z], nz + z, packed)

    col_send[0] = each_z(pack_start, blank)
    pl.semaphore_wait(barrier, gx - 1 + gy - 1)
    send_halo(0)
    v_copies = spread("gx", lambda other: vsend.at[other], lambda slot: vrecv.at[slot],
                      lambda other: v_send.at[other], lambda slot: v_recv.at[slot])
    start(v_copies)

    def magnetic(number, after):
        def body(z, packed):
            ex, ey, ez = elec[0, z], elec[1, z], elec[2, z]
            x_face = row_recv.at[number]
            next_x1 = ahead_x(ey, x_face[0, pl.ds(z, 1)])
            next_x2 = ahead_x(ez, x_face[1, pl.ds(z, 1)])
            cols = col_recv[number]
            next_y0 = ahead_y(ex, cols, z)
            next_y2 = ahead_y(ez, cols, nz + z)
            hx = magn[0, z + 1] - courant * ((next_y2 - ez) - (elec[1, z + 1] - ey))
            hy = magn[1, z + 1] - courant * ((elec[0, z + 1] - ex) - (next_x2 - ez))
            hz = magn[2, z + 1] - courant * ((next_x1 - ey) - (next_y0 - ex))
            magn[0, z + 1] = hx
            magn[1, z + 1] = hy
            magn[2, z + 1] = hz
            row_send[after, 0, pl.ds(z, 1)] = hy[nx - 1:nx]
            row_send[after, 1, pl.ds(z, 1)] = hz[nx - 1:nx]
            return pack_last(hz, nz + z, pack_last(hx, z, packed))
        col_send[after] = each_z(body, blank)

    def curls(field, number, z):
        hx, hy, hz = field[0, z + 1], field[1, z + 1], field[2, z + 1]
        x_face = row_recv.at[number]
        prev_x1 = behind_x(hy, x_face[0, pl.ds(z, 1)])
        prev_x2 = behind_x(hz, x_face[1, pl.ds(z, 1)])
        cols = col_recv[number]
        prev_y0 = behind_y(hx, cols, z)
        prev_y2 = behind_y(hz, cols, nz + z)
        curl_x = (hz - prev_y2) - (hy - field[1, z])
        curl_y = (hx - field[0, z]) - (hz - prev_x2)
        curl_z = (hy - prev_x1) - (hx - prev_y0)
        return curl_x, curl_y, curl_z

    def electric(number, after, tick):
        def body(z, carry):
            packed, plane_x, plane_y = carry
            gain = courant * inv[z]
            curl_x, curl_y, curl_z = curls(magn, number, z)
            ex = elec[0, z] + gain * curl_x
            ey = elec[1, z] + gain * curl_y
            ez = elec[2, z] + gain * curl_z
            elec[0, z] = ex
            elec[1, z] = ey
            elec[2, z] = ez
            seen = mon[...] == z
            plane_x = jnp.where(seen, ex, plane_x)
            plane_y = jnp.where(seen, ey, plane_y)
            if after is not None:
                row_send[after, 0, pl.ds(z, 1)] = ey[0:1]
                row_send[after, 1, pl.ds(z, 1)] = ez[0:1]
                packed = pack_first(ez, nz + z, pack_first(ex, z, packed))
            return packed, plane_x, plane_y
        packed, plane_x, plane_y = each_z(body, (blank, blank, blank))
        if after is not None:
            col_send[after] = packed
        planes[tick, my, 0:nx] = plane_x
        planes[tick, my, nx:2 * nx] = plane_y

    def plane_copies(tick):
        return spread("gy", lambda other: planes.at[tick, my], lambda slot: planes.at[tick, slot],
                      lambda other: p_send.at[tick, other], lambda slot: p_recv.at[tick, slot])

    first_planes, second_planes = plane_copies(0), plane_copies(1)
    g_copies = spread("gy", lambda other: vall.at[my], lambda slot: vall.at[slot],
                      lambda other: g_send.at[other], lambda slot: g_recv.at[slot])
    q_copies = spread("gx", lambda other: qall.at[:, mx], lambda slot: qall.at[:, slot],
                      lambda other: q_send.at[other], lambda slot: q_recv.at[slot])

    loads["h"].wait()
    take_halo(0)
    magnetic(0, 1)
    send_halo(1)

    arrive(v_copies)
    vrecv[mx] = vsend[mx]
    for f in range(freqs):
        total = vrecv[0, f]
        for slot in range(1, gx):
            total = total + vrecv[slot, f]
        top, low = total[0:nx], total[nx:2 * nx]
        for c in range(2):
            vall[my, f, c * nx:(c + 1) * nx] = jnp.concatenate(
                [top[:, c * nb:(c + 1) * nb], low[:, c * nb:(c + 1) * nb]], axis=1)
    start(g_copies)

    for name in ("k", "mon", "src"):
        loads[name].wait()
    take_halo(1)
    electric(1, 2, 0)
    send_halo(2)
    start(first_planes)

    take_halo(2)
    magnetic(2, 3)
    send_halo(3)

    arrive(g_copies)
    loads["back_y"].wait()
    drive = jnp.zeros((2 * nx, len(ticks) * ny), jnp.float32)
    for slot in range(gy):
        for f in range(freqs):
            drive = drive + triple(split(vall[slot, f]), (back_y[slot, f, 0], back_y[slot, f, 1]))

    def adjoint_first(z, packed):
        lit = jnp.where(src[...] == z, (-courant) * inv[z], 0.0)
        ex = lit * drive[0:nx, 0:ny]
        ey = lit * drive[nx:2 * nx, 0:ny]
        aelec[0, z] = ex
        aelec[1, z] = ey
        row_send[4, 0, pl.ds(z, 1)] = ey[0:1]
        return pack_first(ex, z, packed)

    col_send[4] = each_z(adjoint_first, blank)
    send_halo(4)

    take_halo(3)
    electric(3, None, 1)
    start(second_planes)
    stores = [pltpu.make_async_copy(elec.at[:, pl.ds(0, nz)], e_out, out_sems.at[0])]
    stores[0].start()

    take_halo(4)

    def adjoint_magnetic(z, packed):
        ex, ey = aelec[0, z], aelec[1, z]
        next_x1 = ahead_x(ey, row_recv[4, 0, pl.ds(z, 1)])
        next_y0 = ahead_y(ex, col_recv[4], z)
        hx = courant * (aelec[1, z + 1] - ey)
        hy = (-courant) * (aelec[0, z + 1] - ex)
        hz = (-courant) * ((next_x1 - ey) - (next_y0 - ex))
        amagn[0, z + 1] = hx
        amagn[1, z + 1] = hy
        amagn[2, z + 1] = hz
        row_send[5, 0, pl.ds(z, 1)] = hy[nx - 1:nx]
        row_send[5, 1, pl.ds(z, 1)] = hz[nx - 1:nx]
        return pack_last(hz, nz + z, pack_last(hx, z, packed))

    col_send[5] = each_z(adjoint_magnetic, blank)
    send_halo(5)

    loads["far_y"].wait()

    def project(tick):
        total = 0.0
        for slot in range(gy):
            total = total + triple(split(planes[tick, slot]), (far_y[tick, slot, 0], far_y[tick, slot, 1]))
        return total

    arrive(first_planes)
    early = project(0)
    arrive(second_planes)
    half = early + project(1)
    for c in range(2):
        qall[c, mx] = half[c * nx:(c + 1) * nx]
    start(q_copies)

    take_halo(5)

    def adjoint_second(z, carry):
        gain = courant * inv[z]
        curl_x, curl_y, curl_z = curls(amagn, 5, z)
        lit = src[...] == z
        afinal[0, z] = aelec[0, z] + gain * (curl_x - jnp.where(lit, drive[0:nx, ny:2 * ny], 0.0))
        afinal[1, z] = aelec[1, z] + gain * (curl_y - jnp.where(lit, drive[nx:2 * nx, ny:2 * ny], 0.0))
        afinal[2, z] = gain * curl_z
        return carry

    each_z(adjoint_second, 0)
    stores.append(pltpu.make_async_copy(afinal, adj_out, out_sems.at[1]))
    stores[1].start()

    loads["far_x"].wait()
    arrive(q_copies)
    for c in range(2):
        high, low = split(jnp.reshape(qall[c], (gx * nx, freqs * 2 * nb)))
        for f in range(freqs):
            cut = slice(f * 2 * nb, (f + 1) * 2 * nb)
            both = triple((far_x[f, 0], far_x[f, 1]), (high[:, cut], low[:, cut]))
            far[f, c, 0] = both[0:na, 0:nb] + both[na:2 * na, nb:2 * nb]
            far[f, c, 1] = both[0:na, nb:2 * nb] - both[na:2 * na, 0:nb]
    stores.append(pltpu.make_async_copy(far, far_out, out_sems.at[2]))
    stores[2].start()

    for number in range(6):
        end_halo(number)
    for copies in (v_copies, g_copies, first_planes, second_planes, q_copies):
        left(copies)
    for copy in stores:
        copy.wait()


def per_device(consts, gx, gy, e_field, h_field, inverse_permittivity, monitor_layer, source_layer, residual_far):
    _, nz, nx, ny = e_field.shape
    freqs = len(factors)
    na, nb = residual_far.shape[3:]
    f32 = jnp.float32
    shapes = [
        pltpu.VMEM((3, nz + 1, nx, ny), f32),
        pltpu.VMEM((3, nz + 1, nx, ny), f32),
        pltpu.VMEM(inverse_permittivity.shape, f32),
        pltpu.VMEM(monitor_layer.shape, jnp.int32),
        pltpu.VMEM(source_layer.shape, jnp.int32),
        pltpu.VMEM(residual_far.shape, f32),
    ] + [pltpu.VMEM(const.shape[1:], jnp.bfloat16) for const in consts] + [
        pltpu.VMEM((2, nz + 1, nx, ny), f32),
        pltpu.VMEM((3, nz + 1, nx, ny), f32),
        pltpu.VMEM((3, nz, nx, ny), f32),
        pltpu.VMEM(residual_far.shape, f32),
        pltpu.VMEM((6, 2, nz, ny), f32),
        pltpu.VMEM((6, nx, ny), f32),
        pltpu.VMEM((6, 2, nz, ny), f32),
        pltpu.VMEM((6, nx, ny), f32),
        pltpu.VMEM((gx, freqs, 2 * nx, 2 * nb), f32),
        pltpu.VMEM((gx, freqs, 2 * nx, 2 * nb), f32),
        pltpu.VMEM((gy, freqs, 2 * nx, 2 * nb), f32),
        pltpu.VMEM((len(ticks), gy, 2 * nx, ny), f32),
        pltpu.VMEM((2, gx, nx, freqs * 2 * nb), f32),
    ]
    dma = pltpu.SemaphoreType.DMA
    shapes += [dma((10,)), dma((3,)), dma((6, 2)), dma((6, 2)), dma((gx,)), dma((gx,)), dma((gy,)), dma((gy,)),
               dma((len(ticks), gy)), dma((len(ticks), gy)), dma((gx,)), dma((gx,))]
    anywhere = pl.BlockSpec(memory_space=pl.ANY)
    return pl.pallas_call(
        functools.partial(kernel, gx, gy),
        out_shape=(
            jax.ShapeDtypeStruct(e_field.shape, f32),
            jax.ShapeDtypeStruct(residual_far.shape, f32),
            jax.ShapeDtypeStruct(e_field.shape, f32),
        ),
        in_specs=[anywhere] * 10,
        out_specs=(anywhere,) * 3,
        scratch_shapes=shapes,
        compiler_params=pltpu.CompilerParams(
            collective_id=0, has_side_effects=True, vmem_limit_bytes=40 * 1024 * 1024
        ),
    )(e_field, h_field, inverse_permittivity, monitor_layer, source_layer, residual_far, *consts)


def solution(mesh):
    in_specs = (
        P("design", None, "gx", "gy"),
        P("design", None, "gx", "gy"),
        P("design", "gx", "gy"),
        P(("design", "gx"), "gy"),
        P(("design", "gx"), "gy"),
        P("design", None, None, "gx", "gy"),
    )
    out_specs = (
        P("design", None, "gx", "gy"),
        P("design", None, None, "gx", "gy"),
        P("design", None, "gx", "gy"),
    )
    gx, gy = mesh.shape["gx"], mesh.shape["gy"]

    def local(e_field, h_field, inverse_permittivity, monitor_layer, source_layer, residual_far):
        _, _, nx, ny = e_field.shape
        na, nb = residual_far.shape[3:]
        consts = [jnp.asarray(table) for table in tables(gx, gy, na, nb, nx, ny)]
        return per_device(consts, gx, gy, e_field, h_field, inverse_permittivity, monitor_layer,
                          source_layer, residual_far)

    return jax.shard_map(local, mesh=mesh, in_specs=in_specs, out_specs=out_specs, check_vma=False)
```

```python
import functools
import math

import jax
import jax.numpy as jnp
import numpy as np
from jax import lax
from jax.experimental import pallas as pl
from jax.experimental.pallas import tpu as pltpu
from jax.sharding import PartitionSpec as P

courant = 0.5
omegas = (0.7, 1.3)
factors = (3, 5)
MESH = pl.DeviceIdType.MESH
ticks = (1, 2)


def angles(dirs, length):
    rows = np.arange(dirs)[:, None] - dirs // 2
    cols = np.arange(length)[None, :]
    return np.stack(
        [np.mod(rows * cols * factor, 4 * length) * (2.0 * np.pi / (4 * length)) for factor in factors]
    )


def tables(gx, gy, na, nb, nx, ny):
    theta = angles(gx * na, gx * nx)
    phi = angles(gy * nb, gy * ny)
    freqs = len(factors)
    shifted = np.stack([phi + np.array(omegas)[:, None, None] * t for t in ticks])
    both = np.stack([np.cos(shifted), -np.sin(shifted)], axis=2)
    both = both.reshape(len(ticks), freqs, 2, gy, nb, gy, ny)
    far_y = both.transpose(3, 0, 5, 6, 1, 2, 4).reshape(gy, len(ticks), gy, ny, freqs * 2 * nb)
    back_y = both.transpose(5, 3, 1, 2, 4, 0, 6).reshape(gy, gy, freqs, 2 * nb, len(ticks) * ny)
    back_y = back_y / (gx * na)
    pair = np.stack([np.cos(theta), np.sin(theta)], axis=1).reshape(freqs, 2, gx, na, gx * nx)
    far_x = pair.transpose(2, 0, 1, 3, 4).reshape(gx, freqs, 2 * na, gx * nx)
    far_x = far_x / math.sqrt(gx * nx * gy * ny)
    cos, sin = np.cos(theta), np.sin(theta)
    mix = np.stack([np.stack([cos, -sin]), np.stack([sin, cos])])
    mix = mix.reshape(2, 2, freqs, gx, na, gx, nx)
    back_x = mix.transpose(3, 2, 5, 0, 6, 1, 4).reshape(gx, freqs, gx * 2 * nx, 2 * na)
    return [table.astype(np.float32) for table in (far_y, back_y, far_x, back_x)]


def split(value):
    high = value.astype(jnp.bfloat16)
    return high, (value - high.astype(jnp.float32)).astype(jnp.bfloat16)


def mul(left, right):
    return jnp.dot(left, right, preferred_element_type=jnp.float32)


def triple(left, right):
    return mul(left[0], right[0]) + (mul(left[0], right[1]) + mul(left[1], right[0]))


def kernel(
    gx, gy,
    e_in, h_in, k_in, mon_in, src_in, res_in, far_y_in, back_y_in, far_x_in, back_x_in,
    e_out, far_out, adj_out,
    elec, magn, inv, mon, src, res, far_y32, back_y32, far_x, back_x, far_y, back_y,
    aelec, amagn, afinal, far,
    row_send, col_send, row_recv, col_recv,
    vsend, vrecv, vall, planes, qall,
    in_sems, out_sems, halo_send, halo_recv, v_send, v_recv, g_send, g_recv, p_send, p_recv, q_send, q_recv,
):
    mx = lax.axis_index("gx")
    my = lax.axis_index("gy")
    _, nz, nx, ny = e_in.shape
    na, nb = res_in.shape[3:]
    freqs = len(factors)

    loads = {}
    for slot, (name, source, target) in enumerate((
        ("res", res_in, res),
        ("back_x", back_x_in.at[mx], back_x),
        ("e", e_in, elec.at[:, pl.ds(0, nz)]),
        ("h", h_in, magn.at[:, pl.ds(1, nz)]),
        ("k", k_in, inv),
        ("mon", mon_in, mon),
        ("src", src_in, src),
        ("back_y", back_y_in.at[my], back_y32),
        ("far_y", far_y_in.at[my], far_y32),
        ("far_x", far_x_in.at[mx], far_x),
    )):
        loads[name] = pltpu.make_async_copy(source, target, in_sems.at[slot])
        loads[name].start()

    row_recv[...] = jnp.zeros_like(row_recv)
    col_recv[...] = jnp.zeros_like(col_recv)
    blank = jnp.zeros((nx, ny), jnp.float32)
    for part in range(3):
        elec[part, nz] = blank
        magn[part, 0] = blank
        amagn[part, 0] = blank
    for part in range(2):
        aelec[part, nz] = blank

    barrier = pltpu.get_barrier_semaphore()
    for step in range(1, gx):
        pl.semaphore_signal(barrier, inc=1, device_id={"gx": lax.rem(mx + step, gx)}, device_id_type=MESH)
    for step in range(1, gy):
        pl.semaphore_signal(barrier, inc=1, device_id={"gy": lax.rem(my + step, gy)}, device_id_type=MESH)

    lanes = lax.broadcasted_iota(jnp.int32, (nx, ny), 1)
    rows = lax.broadcasted_iota(jnp.int32, (nx, ny), 0)

    def each_z(body, init):
        return lax.fori_loop(0, nz, body, init, unroll=True)

    def ahead_x(value, edge):
        return jnp.where(rows == nx - 1, edge, pltpu.roll(value, nx - 1, axis=0))

    def behind_x(value, edge):
        return jnp.where(rows == 0, edge, pltpu.roll(value, 1, axis=0))

    def ahead_y(value, packed, lane):
        edge = pltpu.roll(packed, lax.rem(2 * ny - 1 - lane, ny), axis=1)
        return jnp.where(lanes == ny - 1, edge, pltpu.roll(value, ny - 1, axis=1))

    def behind_y(value, packed, lane):
        edge = pltpu.roll(packed, lax.rem(2 * ny - lane, ny), axis=1)
        return jnp.where(lanes == 0, edge, pltpu.roll(value, 1, axis=1))

    def pack_first(value, lane, packed):
        return jnp.where(lanes == lane, pltpu.roll(value, lane, axis=1), packed)

    def pack_last(value, lane, packed):
        return jnp.where(lanes == lane, pltpu.roll(value, lane + 1, axis=1), packed)

    def halo(number, direction, count):
        size = gx, gy
        place = mx, my
        out = []
        for which, (axis, send, recv) in enumerate((("gx", row_send, row_recv), ("gy", col_send, col_recv))):
            here, total = place[which], size[which]
            target = lax.rem(here + direction + total, total)
            source_ref = send.at[number, pl.ds(0, count)] if which == 0 else send.at[number]
            target_ref = recv.at[number, pl.ds(0, count)] if which == 0 else recv.at[number]
            copy = pltpu.make_async_remote_copy(
                src_ref=source_ref,
                dst_ref=target_ref,
                send_sem=halo_send.at[number, which],
                recv_sem=halo_recv.at[number, which],
                device_id={axis: target},
                device_id_type=MESH,
            )
            sends = here >= 1 if direction < 0 else here < total - 1
            takes = here < total - 1 if direction < 0 else here >= 1
            out.append((copy, sends, takes))
        return out

    halos = [halo(number, direction, count) for number, (direction, count) in enumerate(
        ((-1, 2), (1, 2), (-1, 2), (1, 2), (-1, 1), (1, 2)))]

    def send_halo(number):
        for copy, sends, _ in halos[number]:
            pl.when(sends)(copy.start)

    def take_halo(number):
        for copy, _, takes in halos[number]:
            pl.when(takes)(copy.wait_recv)

    def end_halo(number):
        for copy, sends, _ in halos[number]:
            pl.when(sends)(copy.wait_send)

    def spread(axis, source, target, send, recv):
        here, total = (mx, gx) if axis == "gx" else (my, gy)
        out = []
        for step in range(1, total):
            other = lax.rem(here + step, total)
            out.append((
                pltpu.make_async_remote_copy(
                    src_ref=source(other), dst_ref=target(here),
                    send_sem=send(other), recv_sem=recv(here),
                    device_id={axis: other}, device_id_type=MESH),
                pltpu.make_async_remote_copy(
                    src_ref=source(other), dst_ref=target(other),
                    send_sem=send(other), recv_sem=recv(other),
                    device_id={axis: other}, device_id_type=MESH),
            ))
        return out

    def start(copies):
        for copy, _ in copies:
            copy.start()

    def arrive(copies):
        for _, copy in copies:
            copy.wait_recv()

    def left(copies):
        for copy, _ in copies:
            copy.wait_send()

    loads["res"].wait()
    loads["back_x"].wait()
    for f in range(freqs):
        block = jnp.concatenate(
            [jnp.concatenate([res[f, c, 0], res[f, c, 1]], axis=0) for c in range(2)], axis=1)
        part = triple(split(back_x[f]), split(block))
        for other in range(gx):
            vsend[other, f] = part[other * 2 * nx:(other + 1) * 2 * nx]

    loads["e"].wait()

    def pack_start(z, packed):
        row_send[0, 0, pl.ds(z, 1)] = elec[1, z, 0:1]
        row_send[0, 1, pl.ds(z, 1)] = elec[2, z, 0:1]
        packed = pack_first(elec[0, z], z, packed)
        return pack_first(elec[2, z], nz + z, packed)

    col_send[0] = each_z(pack_start, blank)
    pl.semaphore_wait(barrier, gx - 1 + gy - 1)
    send_halo(0)
    v_copies = spread("gx", lambda other: vsend.at[other], lambda slot: vrecv.at[slot],
                      lambda other: v_send.at[other], lambda slot: v_recv.at[slot])
    start(v_copies)

    loads["back_y"].wait()
    for slot in range(gy):
        for f in range(freqs):
            back_y[slot, f, 0], back_y[slot, f, 1] = split(back_y32[slot, f])
    loads["far_y"].wait()
    for tick in range(len(ticks)):
        for slot in range(gy):
            far_y[tick, slot, 0], far_y[tick, slot, 1] = split(far_y32[tick, slot])

    def magnetic(number, after):
        def body(z, packed):
            ex, ey, ez = elec[0, z], elec[1, z], elec[2, z]
            x_face = row_recv.at[number]
            next_x1 = ahead_x(ey, x_face[0, pl.ds(z, 1)])
            next_x2 = ahead_x(ez, x_face[1, pl.ds(z, 1)])
            cols = col_recv[number]
            next_y0 = ahead_y(ex, cols, z)
            next_y2 = ahead_y(ez, cols, nz + z)
            hx = magn[0, z + 1] - courant * ((next_y2 - ez) - (elec[1, z + 1] - ey))
            hy = magn[1, z + 1] - courant * ((elec[0, z + 1] - ex) - (next_x2 - ez))
            hz = magn[2, z + 1] - courant * ((next_x1 - ey) - (next_y0 - ex))
            magn[0, z + 1] = hx
            magn[1, z + 1] = hy
            magn[2, z + 1] = hz
            row_send[after, 0, pl.ds(z, 1)] = hy[nx - 1:nx]
            row_send[after, 1, pl.ds(z, 1)] = hz[nx - 1:nx]
            return pack_last(hz, nz + z, pack_last(hx, z, packed))
        col_send[after] = each_z(body, blank)

    def curls(field, number, z):
        hx, hy, hz = field[0, z + 1], field[1, z + 1], field[2, z + 1]
        x_face = row_recv.at[number]
        prev_x1 = behind_x(hy, x_face[0, pl.ds(z, 1)])
        prev_x2 = behind_x(hz, x_face[1, pl.ds(z, 1)])
        cols = col_recv[number]
        prev_y0 = behind_y(hx, cols, z)
        prev_y2 = behind_y(hz, cols, nz + z)
        curl_x = (hz - prev_y2) - (hy - field[1, z])
        curl_y = (hx - field[0, z]) - (hz - prev_x2)
        curl_z = (hy - prev_x1) - (hx - prev_y0)
        return curl_x, curl_y, curl_z

    def electric(number, after, tick):
        def body(z, carry):
            packed, plane_x, plane_y = carry
            gain = courant * inv[z]
            curl_x, curl_y, curl_z = curls(magn, number, z)
            ex = elec[0, z] + gain * curl_x
            ey = elec[1, z] + gain * curl_y
            ez = elec[2, z] + gain * curl_z
            elec[0, z] = ex
            elec[1, z] = ey
            elec[2, z] = ez
            seen = mon[...] == z
            plane_x = jnp.where(seen, ex, plane_x)
            plane_y = jnp.where(seen, ey, plane_y)
            if after is not None:
                row_send[after, 0, pl.ds(z, 1)] = ey[0:1]
                row_send[after, 1, pl.ds(z, 1)] = ez[0:1]
                packed = pack_first(ez, nz + z, pack_first(ex, z, packed))
            return packed, plane_x, plane_y
        packed, plane_x, plane_y = each_z(body, (blank, blank, blank))
        if after is not None:
            col_send[after] = packed
        planes[tick, my, 0:nx] = plane_x
        planes[tick, my, nx:2 * nx] = plane_y

    def plane_copies(tick):
        return spread("gy", lambda other: planes.at[tick, my], lambda slot: planes.at[tick, slot],
                      lambda other: p_send.at[tick, other], lambda slot: p_recv.at[tick, slot])

    first_planes, second_planes = plane_copies(0), plane_copies(1)
    g_copies = spread("gy", lambda other: vall.at[my], lambda slot: vall.at[slot],
                      lambda other: g_send.at[other], lambda slot: g_recv.at[slot])
    q_copies = spread("gx", lambda other: qall.at[:, mx], lambda slot: qall.at[:, slot],
                      lambda other: q_send.at[other], lambda slot: q_recv.at[slot])

    loads["h"].wait()
    take_halo(0)
    magnetic(0, 1)
    send_halo(1)

    arrive(v_copies)
    vrecv[mx] = vsend[mx]
    for f in range(freqs):
        total = vrecv[0, f]
        for slot in range(1, gx):
            total = total + vrecv[slot, f]
        top, low = total[0:nx], total[nx:2 * nx]
        for c in range(2):
            vall[my, f, c * nx:(c + 1) * nx] = jnp.concatenate(
                [top[:, c * nb:(c + 1) * nb], low[:, c * nb:(c + 1) * nb]], axis=1)
    start(g_copies)

    for name in ("k", "mon", "src"):
        loads[name].wait()
    take_halo(1)
    electric(1, 2, 0)
    send_halo(2)
    start(first_planes)

    take_halo(2)
    magnetic(2, 3)
    send_halo(3)

    arrive(g_copies)
    drive = jnp.zeros((2 * nx, len(ticks) * ny), jnp.float32)
    for slot in range(gy):
        for f in range(freqs):
            drive = drive + triple(split(vall[slot, f]), (back_y[slot, f, 0], back_y[slot, f, 1]))

    def adjoint_first(z, packed):
        lit = jnp.where(src[...] == z, (-courant) * inv[z], 0.0)
        ex = lit * drive[0:nx, 0:ny]
        ey = lit * drive[nx:2 * nx, 0:ny]
        aelec[0, z] = ex
        aelec[1, z] = ey
        row_send[4, 0, pl.ds(z, 1)] = ey[0:1]
        return pack_first(ex, z, packed)

    col_send[4] = each_z(adjoint_first, blank)
    send_halo(4)

    take_halo(3)
    electric(3, None, 1)
    start(second_planes)
    stores = [pltpu.make_async_copy(elec.at[:, pl.ds(0, nz)], e_out, out_sems.at[0])]
    stores[0].start()

    take_halo(4)

    def adjoint_magnetic(z, packed):
        ex, ey = aelec[0, z], aelec[1, z]
        next_x1 = ahead_x(ey, row_recv[4, 0, pl.ds(z, 1)])
        next_y0 = ahead_y(ex, col_recv[4], z)
        hx = courant * (aelec[1, z + 1] - ey)
        hy = (-courant) * (aelec[0, z + 1] - ex)
        hz = (-courant) * ((next_x1 - ey) - (next_y0 - ex))
        amagn[0, z + 1] = hx
        amagn[1, z + 1] = hy
        amagn[2, z + 1] = hz
        row_send[5, 0, pl.ds(z, 1)] = hy[nx - 1:nx]
        row_send[5, 1, pl.ds(z, 1)] = hz[nx - 1:nx]
        return pack_last(hz, nz + z, pack_last(hx, z, packed))

    col_send[5] = each_z(adjoint_magnetic, blank)
    send_halo(5)

    def project(tick):
        total = 0.0
        for slot in range(gy):
            total = total + triple(split(planes[tick, slot]), (far_y[tick, slot, 0], far_y[tick, slot, 1]))
        return total

    arrive(first_planes)
    early = project(0)
    arrive(second_planes)
    half = early + project(1)
    for c in range(2):
        qall[c, mx] = half[c * nx:(c + 1) * nx]
    start(q_copies)

    take_halo(5)

    def adjoint_second(z, carry):
        gain = courant * inv[z]
        curl_x, curl_y, curl_z = curls(amagn, 5, z)
        lit = src[...] == z
        afinal[0, z] = aelec[0, z] + gain * (curl_x - jnp.where(lit, drive[0:nx, ny:2 * ny], 0.0))
        afinal[1, z] = aelec[1, z] + gain * (curl_y - jnp.where(lit, drive[nx:2 * nx, ny:2 * ny], 0.0))
        afinal[2, z] = gain * curl_z
        return carry

    each_z(adjoint_second, 0)
    stores.append(pltpu.make_async_copy(afinal, adj_out, out_sems.at[1]))
    stores[1].start()

    loads["far_x"].wait()
    arrive(q_copies)
    for c in range(2):
        high, low = split(jnp.reshape(qall[c], (gx * nx, freqs * 2 * nb)))
        for f in range(freqs):
            cut = slice(f * 2 * nb, (f + 1) * 2 * nb)
            both = triple(split(far_x[f]), (high[:, cut], low[:, cut]))
            far[f, c, 0] = both[0:na, 0:nb] + both[na:2 * na, nb:2 * nb]
            far[f, c, 1] = both[0:na, nb:2 * nb] - both[na:2 * na, 0:nb]
    stores.append(pltpu.make_async_copy(far, far_out, out_sems.at[2]))
    stores[2].start()

    for number in range(6):
        end_halo(number)
    for copies in (v_copies, g_copies, first_planes, second_planes, q_copies):
        left(copies)
    for copy in stores:
        copy.wait()


def hand_out(e_made, far_made, adj_made, e_out, far_out, adj_out, sems):
    copies = []
    for made, out in ((e_made, e_out), (far_made, far_out), (adj_made, adj_out)):
        for part in range(made.shape[0]):
            copies.append(pltpu.make_async_copy(made.at[part], out.at[part], sems.at[len(copies)]))
    for copy in copies:
        copy.start()
    for copy in copies:
        copy.wait()


def per_device(consts, gx, gy, e_field, h_field, inverse_permittivity, monitor_layer, source_layer, residual_far):
    _, nz, nx, ny = e_field.shape
    freqs = len(factors)
    na, nb = residual_far.shape[3:]
    f32 = jnp.float32
    shapes = [
        pltpu.VMEM((3, nz + 1, nx, ny), f32),
        pltpu.VMEM((3, nz + 1, nx, ny), f32),
        pltpu.VMEM(inverse_permittivity.shape, f32),
        pltpu.VMEM(monitor_layer.shape, jnp.int32),
        pltpu.VMEM(source_layer.shape, jnp.int32),
        pltpu.VMEM(residual_far.shape, f32),
    ] + [pltpu.VMEM(const.shape[1:], f32) for const in consts] + [
        pltpu.VMEM(const.shape[1:-2] + (2,) + const.shape[-2:], jnp.bfloat16) for const in consts[:2]
    ] + [
        pltpu.VMEM((2, nz + 1, nx, ny), f32),
        pltpu.VMEM((3, nz + 1, nx, ny), f32),
        pltpu.VMEM((3, nz, nx, ny), f32),
        pltpu.VMEM(residual_far.shape, f32),
        pltpu.VMEM((6, 2, nz, ny), f32),
        pltpu.VMEM((6, nx, ny), f32),
        pltpu.VMEM((6, 2, nz, ny), f32),
        pltpu.VMEM((6, nx, ny), f32),
        pltpu.VMEM((gx, freqs, 2 * nx, 2 * nb), f32),
        pltpu.VMEM((gx, freqs, 2 * nx, 2 * nb), f32),
        pltpu.VMEM((gy, freqs, 2 * nx, 2 * nb), f32),
        pltpu.VMEM((len(ticks), gy, 2 * nx, ny), f32),
        pltpu.VMEM((2, gx, nx, freqs * 2 * nb), f32),
    ]
    dma = pltpu.SemaphoreType.DMA
    shapes += [dma((10,)), dma((3,)), dma((6, 2)), dma((6, 2)), dma((gx,)), dma((gx,)), dma((gy,)), dma((gy,)),
               dma((len(ticks), gy)), dma((len(ticks), gy)), dma((gx,)), dma((gx,))]
    anywhere = pl.BlockSpec(memory_space=pl.ANY)
    main = pl.BlockSpec(memory_space=pltpu.HBM)
    out_shape = (
        jax.ShapeDtypeStruct(e_field.shape, f32),
        jax.ShapeDtypeStruct(residual_far.shape, f32),
        jax.ShapeDtypeStruct(e_field.shape, f32),
    )
    results = pl.pallas_call(
        functools.partial(kernel, gx, gy),
        out_shape=out_shape,
        in_specs=[main] * 10,
        out_specs=(anywhere,) * 3,
        scratch_shapes=shapes,
        compiler_params=pltpu.CompilerParams(
            collective_id=0, has_side_effects=True, vmem_limit_bytes=64 * 1024 * 1024
        ),
    )(e_field, h_field, inverse_permittivity, monitor_layer, source_layer, residual_far, *consts)
    return pl.pallas_call(
        hand_out,
        out_shape=out_shape,
        in_specs=[anywhere] * 3,
        out_specs=(main,) * 3,
        scratch_shapes=[dma((3 + freqs + 3,))],
        compiler_params=pltpu.CompilerParams(vmem_limit_bytes=64 * 1024 * 1024),
    )(*results)


def solution(mesh):
    in_specs = (
        P("design", None, "gx", "gy"),
        P("design", None, "gx", "gy"),
        P("design", "gx", "gy"),
        P(("design", "gx"), "gy"),
        P(("design", "gx"), "gy"),
        P("design", None, None, "gx", "gy"),
    )
    out_specs = (
        P("design", None, "gx", "gy"),
        P("design", None, None, "gx", "gy"),
        P("design", None, "gx", "gy"),
    )
    gx, gy = mesh.shape["gx"], mesh.shape["gy"]

    def local(e_field, h_field, inverse_permittivity, monitor_layer, source_layer, residual_far):
        _, _, nx, ny = e_field.shape
        na, nb = residual_far.shape[3:]
        consts = [jnp.asarray(table) for table in tables(gx, gy, na, nb, nx, ny)]
        return per_device(consts, gx, gy, e_field, h_field, inverse_permittivity, monitor_layer,
                          source_layer, residual_far)

    return jax.shard_map(local, mesh=mesh, in_specs=in_specs, out_specs=out_specs, check_vma=False)
```

```python
import functools
import math

import jax
import jax.numpy as jnp
import numpy as np
from jax import lax
from jax.experimental import pallas as pl
from jax.experimental.pallas import tpu as pltpu
from jax.sharding import PartitionSpec as P

courant = 0.5
omegas = (0.7, 1.3)
factors = (3, 5)
MESH = pl.DeviceIdType.MESH
ticks = (1, 2)


def angles(dirs, length):
    rows = np.arange(dirs)[:, None] - dirs // 2
    cols = np.arange(length)[None, :]
    return np.stack(
        [np.mod(rows * cols * factor, 4 * length) * (2.0 * np.pi / (4 * length)) for factor in factors]
    )


def tables(gx, gy, na, nb, nx, ny):
    theta = angles(gx * na, gx * nx)
    phi = angles(gy * nb, gy * ny)
    freqs = len(factors)
    shifted = np.stack([phi + np.array(omegas)[:, None, None] * t for t in ticks])
    both = np.stack([np.cos(shifted), -np.sin(shifted)], axis=2)
    both = both.reshape(len(ticks), freqs, 2, gy, nb, gy, ny)
    far_y = both.transpose(3, 0, 5, 6, 1, 2, 4).reshape(gy, len(ticks), gy, ny, freqs * 2 * nb)
    back_y = both.transpose(5, 3, 1, 2, 4, 0, 6).reshape(gy, gy, freqs, 2 * nb, len(ticks) * ny)
    back_y = back_y / (gx * na)
    pair = np.stack([np.cos(theta), np.sin(theta)], axis=1).reshape(freqs, 2, gx, na, gx * nx)
    far_x = pair.transpose(2, 0, 1, 3, 4).reshape(gx, freqs, 2 * na, gx * nx)
    far_x = far_x / math.sqrt(gx * nx * gy * ny)
    cos, sin = np.cos(theta), np.sin(theta)
    mix = np.stack([np.stack([cos, -sin]), np.stack([sin, cos])])
    mix = mix.reshape(2, 2, freqs, gx, na, gx, nx)
    back_x = mix.transpose(3, 2, 5, 0, 6, 1, 4).reshape(gx, freqs, gx * 2 * nx, 2 * na)
    return [table.astype(np.float32) for table in (far_y, back_y, far_x, back_x)]


def split(value):
    high = value.astype(jnp.bfloat16)
    return high, (value - high.astype(jnp.float32)).astype(jnp.bfloat16)


def mul(left, right):
    return jnp.dot(left, right, preferred_element_type=jnp.float32)


def triple(left, right):
    return mul(left[0], right[0]) + (mul(left[0], right[1]) + mul(left[1], right[0]))


def kernel(
    gx, gy,
    e_in, h_in, k_in, mon_in, src_in, res_in, far_y_in, back_y_in, far_x_in, back_x_in,
    e_out, far_out, adj_out,
    elec, magn, inv, mon, src, res, far_y32, back_y32, far_x, back_x, far_y, back_y,
    aelec, amagn, afinal, far,
    row_send, col_send, row_recv, col_recv,
    vsend, vrecv, vall, planes, qall,
    in_sems, out_sems, halo_send, halo_recv, v_send, v_recv, g_send, g_recv, p_send, p_recv, q_send, q_recv,
):
    mx = lax.axis_index("gx")
    my = lax.axis_index("gy")
    _, nz, nx, ny = e_in.shape
    na, nb = res_in.shape[3:]
    freqs = len(factors)

    loads = {}
    for slot, (name, source, target) in enumerate((
        ("res", res_in, res),
        ("back_x", back_x_in.at[mx], back_x),
        ("e", e_in, elec.at[:, pl.ds(0, nz)]),
        ("h", h_in, magn.at[:, pl.ds(1, nz)]),
        ("k", k_in, inv),
        ("mon", mon_in, mon),
        ("src", src_in, src),
        ("back_y", back_y_in.at[my], back_y32),
        ("far_y", far_y_in.at[my], far_y32),
        ("far_x", far_x_in.at[mx], far_x),
    )):
        loads[name] = pltpu.make_async_copy(source, target, in_sems.at[slot])
        loads[name].start()

    row_recv[...] = jnp.zeros_like(row_recv)
    col_recv[...] = jnp.zeros_like(col_recv)
    blank = jnp.zeros((nx, ny), jnp.float32)
    for part in range(3):
        elec[part, nz] = blank
        magn[part, 0] = blank
        amagn[part, 0] = blank
    for part in range(2):
        aelec[part, nz] = blank

    barrier = pltpu.get_barrier_semaphore()
    for step in range(1, gx):
        pl.semaphore_signal(barrier, inc=1, device_id={"gx": lax.rem(mx + step, gx)}, device_id_type=MESH)
    for step in range(1, gy):
        pl.semaphore_signal(barrier, inc=1, device_id={"gy": lax.rem(my + step, gy)}, device_id_type=MESH)

    lanes = lax.broadcasted_iota(jnp.int32, (nx, ny), 1)
    rows = lax.broadcasted_iota(jnp.int32, (nx, ny), 0)

    def each_z(body, init):
        return lax.fori_loop(0, nz, body, init, unroll=True)

    def ahead_x(value, edge):
        return jnp.where(rows == nx - 1, edge, pltpu.roll(value, nx - 1, axis=0))

    def behind_x(value, edge):
        return jnp.where(rows == 0, edge, pltpu.roll(value, 1, axis=0))

    def ahead_y(value, packed, lane):
        edge = pltpu.roll(packed, lax.rem(2 * ny - 1 - lane, ny), axis=1)
        return jnp.where(lanes == ny - 1, edge, pltpu.roll(value, ny - 1, axis=1))

    def behind_y(value, packed, lane):
        edge = pltpu.roll(packed, lax.rem(2 * ny - lane, ny), axis=1)
        return jnp.where(lanes == 0, edge, pltpu.roll(value, 1, axis=1))

    def pack_first(value, lane, packed):
        return jnp.where(lanes == lane, pltpu.roll(value, lane, axis=1), packed)

    def pack_last(value, lane, packed):
        return jnp.where(lanes == lane, pltpu.roll(value, lane + 1, axis=1), packed)

    def halo(number, direction, count):
        size = gx, gy
        place = mx, my
        out = []
        for which, (axis, send, recv) in enumerate((("gx", row_send, row_recv), ("gy", col_send, col_recv))):
            here, total = place[which], size[which]
            target = lax.rem(here + direction + total, total)
            source_ref = send.at[number, pl.ds(0, count)] if which == 0 else send.at[number]
            target_ref = recv.at[number, pl.ds(0, count)] if which == 0 else recv.at[number]
            copy = pltpu.make_async_remote_copy(
                src_ref=source_ref,
                dst_ref=target_ref,
                send_sem=halo_send.at[number, which],
                recv_sem=halo_recv.at[number, which],
                device_id={axis: target},
                device_id_type=MESH,
            )
            sends = here >= 1 if direction < 0 else here < total - 1
            takes = here < total - 1 if direction < 0 else here >= 1
            out.append((copy, sends, takes))
        return out

    halos = [halo(number, direction, count) for number, (direction, count) in enumerate(
        ((-1, 2), (1, 2), (-1, 2), (1, 2), (-1, 1), (1, 2)))]

    def send_halo(number):
        for copy, sends, _ in halos[number]:
            pl.when(sends)(copy.start)

    def take_halo(number):
        for copy, _, takes in halos[number]:
            pl.when(takes)(copy.wait_recv)

    def end_halo(number):
        for copy, sends, _ in halos[number]:
            pl.when(sends)(copy.wait_send)

    def spread(axis, source, target, send, recv):
        here, total = (mx, gx) if axis == "gx" else (my, gy)
        out = []
        for step in range(1, total):
            other = lax.rem(here + step, total)
            out.append((
                pltpu.make_async_remote_copy(
                    src_ref=source(other), dst_ref=target(here),
                    send_sem=send(other), recv_sem=recv(here),
                    device_id={axis: other}, device_id_type=MESH),
                pltpu.make_async_remote_copy(
                    src_ref=source(other), dst_ref=target(other),
                    send_sem=send(other), recv_sem=recv(other),
                    device_id={axis: other}, device_id_type=MESH),
            ))
        return out

    def start(copies):
        for copy, _ in copies:
            copy.start()

    def arrive(copies):
        for _, copy in copies:
            copy.wait_recv()

    def left(copies):
        for copy, _ in copies:
            copy.wait_send()

    loads["res"].wait()
    loads["back_x"].wait()
    for f in range(freqs):
        block = jnp.concatenate(
            [jnp.concatenate([res[f, c, 0], res[f, c, 1]], axis=0) for c in range(2)], axis=1)
        part = triple(split(back_x[f]), split(block))
        for other in range(gx):
            vsend[other, f] = part[other * 2 * nx:(other + 1) * 2 * nx]

    loads["e"].wait()

    def pack_start(z, packed):
        row_send[0, 0, pl.ds(z, 1)] = elec[1, z, 0:1]
        row_send[0, 1, pl.ds(z, 1)] = elec[2, z, 0:1]
        packed = pack_first(elec[0, z], z, packed)
        return pack_first(elec[2, z], nz + z, packed)

    col_send[0] = each_z(pack_start, blank)
    pl.semaphore_wait(barrier, gx - 1 + gy - 1)
    send_halo(0)
    v_copies = spread("gx", lambda other: vsend.at[other], lambda slot: vrecv.at[slot],
                      lambda other: v_send.at[other], lambda slot: v_recv.at[slot])
    start(v_copies)

    loads["back_y"].wait()
    for slot in range(gy):
        for f in range(freqs):
            back_y[slot, f, 0], back_y[slot, f, 1] = split(back_y32[slot, f])
    loads["far_y"].wait()
    for tick in range(len(ticks)):
        for slot in range(gy):
            far_y[tick, slot, 0], far_y[tick, slot, 1] = split(far_y32[tick, slot])

    def magnetic(number, after):
        def body(z, packed):
            ex, ey, ez = elec[0, z], elec[1, z], elec[2, z]
            x_face = row_recv.at[number]
            next_x1 = ahead_x(ey, x_face[0, pl.ds(z, 1)])
            next_x2 = ahead_x(ez, x_face[1, pl.ds(z, 1)])
            cols = col_recv[number]
            next_y0 = ahead_y(ex, cols, z)
            next_y2 = ahead_y(ez, cols, nz + z)
            hx = magn[0, z + 1] - courant * ((next_y2 - ez) - (elec[1, z + 1] - ey))
            hy = magn[1, z + 1] - courant * ((elec[0, z + 1] - ex) - (next_x2 - ez))
            hz = magn[2, z + 1] - courant * ((next_x1 - ey) - (next_y0 - ex))
            magn[0, z + 1] = hx
            magn[1, z + 1] = hy
            magn[2, z + 1] = hz
            row_send[after, 0, pl.ds(z, 1)] = hy[nx - 1:nx]
            row_send[after, 1, pl.ds(z, 1)] = hz[nx - 1:nx]
            return pack_last(hz, nz + z, pack_last(hx, z, packed))
        col_send[after] = each_z(body, blank)

    def curls(field, number, z):
        hx, hy, hz = field[0, z + 1], field[1, z + 1], field[2, z + 1]
        x_face = row_recv.at[number]
        prev_x1 = behind_x(hy, x_face[0, pl.ds(z, 1)])
        prev_x2 = behind_x(hz, x_face[1, pl.ds(z, 1)])
        cols = col_recv[number]
        prev_y0 = behind_y(hx, cols, z)
        prev_y2 = behind_y(hz, cols, nz + z)
        curl_x = (hz - prev_y2) - (hy - field[1, z])
        curl_y = (hx - field[0, z]) - (hz - prev_x2)
        curl_z = (hy - prev_x1) - (hx - prev_y0)
        return curl_x, curl_y, curl_z

    def electric(number, after, tick):
        def body(z, carry):
            packed, plane_x, plane_y = carry
            gain = courant * inv[z]
            curl_x, curl_y, curl_z = curls(magn, number, z)
            ex = elec[0, z] + gain * curl_x
            ey = elec[1, z] + gain * curl_y
            ez = elec[2, z] + gain * curl_z
            elec[0, z] = ex
            elec[1, z] = ey
            elec[2, z] = ez
            seen = mon[...] == z
            plane_x = jnp.where(seen, ex, plane_x)
            plane_y = jnp.where(seen, ey, plane_y)
            if after is not None:
                row_send[after, 0, pl.ds(z, 1)] = ey[0:1]
                row_send[after, 1, pl.ds(z, 1)] = ez[0:1]
                packed = pack_first(ez, nz + z, pack_first(ex, z, packed))
            return packed, plane_x, plane_y
        packed, plane_x, plane_y = each_z(body, (blank, blank, blank))
        if after is not None:
            col_send[after] = packed
        planes[tick, my, 0:nx] = plane_x
        planes[tick, my, nx:2 * nx] = plane_y

    def plane_copies(tick):
        return spread("gy", lambda other: planes.at[tick, my], lambda slot: planes.at[tick, slot],
                      lambda other: p_send.at[tick, other], lambda slot: p_recv.at[tick, slot])

    first_planes, second_planes = plane_copies(0), plane_copies(1)
    g_copies = spread("gy", lambda other: vall.at[my], lambda slot: vall.at[slot],
                      lambda other: g_send.at[other], lambda slot: g_recv.at[slot])
    q_copies = spread("gx", lambda other: qall.at[:, mx], lambda slot: qall.at[:, slot],
                      lambda other: q_send.at[other], lambda slot: q_recv.at[slot])

    loads["h"].wait()
    take_halo(0)
    magnetic(0, 1)
    send_halo(1)

    arrive(v_copies)
    vrecv[mx] = vsend[mx]
    for f in range(freqs):
        total = vrecv[0, f]
        for slot in range(1, gx):
            total = total + vrecv[slot, f]
        top, low = total[0:nx], total[nx:2 * nx]
        for c in range(2):
            vall[my, f, c * nx:(c + 1) * nx] = jnp.concatenate(
                [top[:, c * nb:(c + 1) * nb], low[:, c * nb:(c + 1) * nb]], axis=1)
    start(g_copies)

    for name in ("k", "mon", "src"):
        loads[name].wait()
    take_halo(1)
    electric(1, 2, 0)
    send_halo(2)
    start(first_planes)

    take_halo(2)
    magnetic(2, 3)
    send_halo(3)

    arrive(g_copies)
    drive = jnp.zeros((2 * nx, len(ticks) * ny), jnp.float32)
    for slot in range(gy):
        for f in range(freqs):
            drive = drive + triple(split(vall[slot, f]), (back_y[slot, f, 0], back_y[slot, f, 1]))

    def adjoint_first(z, packed):
        lit = jnp.where(src[...] == z, (-courant) * inv[z], 0.0)
        ex = lit * drive[0:nx, 0:ny]
        ey = lit * drive[nx:2 * nx, 0:ny]
        aelec[0, z] = ex
        aelec[1, z] = ey
        row_send[4, 0, pl.ds(z, 1)] = ey[0:1]
        return pack_first(ex, z, packed)

    col_send[4] = each_z(adjoint_first, blank)
    send_halo(4)

    take_halo(3)
    electric(3, None, 1)
    start(second_planes)
    stores = [pltpu.make_async_copy(elec.at[:, pl.ds(0, nz)], e_out, out_sems.at[0])]
    stores[0].start()

    take_halo(4)

    def adjoint_magnetic(z, packed):
        ex, ey = aelec[0, z], aelec[1, z]
        next_x1 = ahead_x(ey, row_recv[4, 0, pl.ds(z, 1)])
        next_y0 = ahead_y(ex, col_recv[4], z)
        hx = courant * (aelec[1, z + 1] - ey)
        hy = (-courant) * (aelec[0, z + 1] - ex)
        hz = (-courant) * ((next_x1 - ey) - (next_y0 - ex))
        amagn[0, z + 1] = hx
        amagn[1, z + 1] = hy
        amagn[2, z + 1] = hz
        row_send[5, 0, pl.ds(z, 1)] = hy[nx - 1:nx]
        row_send[5, 1, pl.ds(z, 1)] = hz[nx - 1:nx]
        return pack_last(hz, nz + z, pack_last(hx, z, packed))

    col_send[5] = each_z(adjoint_magnetic, blank)
    send_halo(5)

    def project(tick):
        total = 0.0
        for slot in range(gy):
            total = total + triple(split(planes[tick, slot]), (far_y[tick, slot, 0], far_y[tick, slot, 1]))
        return total

    arrive(first_planes)
    early = project(0)
    arrive(second_planes)
    half = early + project(1)
    for c in range(2):
        qall[c, mx] = half[c * nx:(c + 1) * nx]
    start(q_copies)

    take_halo(5)

    def adjoint_second(z, carry):
        gain = courant * inv[z]
        curl_x, curl_y, curl_z = curls(amagn, 5, z)
        lit = src[...] == z
        afinal[0, z] = aelec[0, z] + gain * (curl_x - jnp.where(lit, drive[0:nx, ny:2 * ny], 0.0))
        afinal[1, z] = aelec[1, z] + gain * (curl_y - jnp.where(lit, drive[nx:2 * nx, ny:2 * ny], 0.0))
        afinal[2, z] = gain * curl_z
        return carry

    each_z(adjoint_second, 0)
    stores.append(pltpu.make_async_copy(afinal, adj_out, out_sems.at[1]))
    stores[1].start()

    loads["far_x"].wait()
    arrive(q_copies)
    for c in range(2):
        high, low = split(jnp.reshape(qall[c], (gx * nx, freqs * 2 * nb)))
        for f in range(freqs):
            cut = slice(f * 2 * nb, (f + 1) * 2 * nb)
            both = triple(split(far_x[f]), (high[:, cut], low[:, cut]))
            far[f, c, 0] = both[0:na, 0:nb] + both[na:2 * na, nb:2 * nb]
            far[f, c, 1] = both[0:na, nb:2 * nb] - both[na:2 * na, 0:nb]
    stores.append(pltpu.make_async_copy(far, far_out, out_sems.at[2]))
    stores[2].start()

    for number in range(6):
        end_halo(number)
    for copies in (v_copies, g_copies, first_planes, second_planes, q_copies):
        left(copies)
    for copy in stores:
        copy.wait()


def hand_out(e_made, far_made, adj_made, e_out, far_out, adj_out, e_held, far_held, adj_held, load_sems, store_sems):
    moves = []
    for made, held, out in ((e_made, e_held, e_out), (far_made, far_held, far_out), (adj_made, adj_held, adj_out)):
        for part in range(made.shape[0]):
            slot = len(moves)
            moves.append((
                pltpu.make_async_copy(made.at[part], held.at[part], load_sems.at[slot]),
                pltpu.make_async_copy(held.at[part], out.at[part], store_sems.at[slot]),
            ))
    for load, _ in moves:
        load.start()
    for load, store in moves:
        load.wait()
        store.start()
    for _, store in moves:
        store.wait()


def per_device(consts, gx, gy, e_field, h_field, inverse_permittivity, monitor_layer, source_layer, residual_far):
    _, nz, nx, ny = e_field.shape
    freqs = len(factors)
    na, nb = residual_far.shape[3:]
    f32 = jnp.float32
    shapes = [
        pltpu.VMEM((3, nz + 1, nx, ny), f32),
        pltpu.VMEM((3, nz + 1, nx, ny), f32),
        pltpu.VMEM(inverse_permittivity.shape, f32),
        pltpu.VMEM(monitor_layer.shape, jnp.int32),
        pltpu.VMEM(source_layer.shape, jnp.int32),
        pltpu.VMEM(residual_far.shape, f32),
    ] + [pltpu.VMEM(const.shape[1:], f32) for const in consts] + [
        pltpu.VMEM(const.shape[1:-2] + (2,) + const.shape[-2:], jnp.bfloat16) for const in consts[:2]
    ] + [
        pltpu.VMEM((2, nz + 1, nx, ny), f32),
        pltpu.VMEM((3, nz + 1, nx, ny), f32),
        pltpu.VMEM((3, nz, nx, ny), f32),
        pltpu.VMEM(residual_far.shape, f32),
        pltpu.VMEM((6, 2, nz, ny), f32),
        pltpu.VMEM((6, nx, ny), f32),
        pltpu.VMEM((6, 2, nz, ny), f32),
        pltpu.VMEM((6, nx, ny), f32),
        pltpu.VMEM((gx, freqs, 2 * nx, 2 * nb), f32),
        pltpu.VMEM((gx, freqs, 2 * nx, 2 * nb), f32),
        pltpu.VMEM((gy, freqs, 2 * nx, 2 * nb), f32),
        pltpu.VMEM((len(ticks), gy, 2 * nx, ny), f32),
        pltpu.VMEM((2, gx, nx, freqs * 2 * nb), f32),
    ]
    dma = pltpu.SemaphoreType.DMA
    shapes += [dma((10,)), dma((3,)), dma((6, 2)), dma((6, 2)), dma((gx,)), dma((gx,)), dma((gy,)), dma((gy,)),
               dma((len(ticks), gy)), dma((len(ticks), gy)), dma((gx,)), dma((gx,))]
    anywhere = pl.BlockSpec(memory_space=pl.ANY)
    main = pl.BlockSpec(memory_space=pltpu.HBM)
    out_shape = (
        jax.ShapeDtypeStruct(e_field.shape, f32),
        jax.ShapeDtypeStruct(residual_far.shape, f32),
        jax.ShapeDtypeStruct(e_field.shape, f32),
    )
    results = pl.pallas_call(
        functools.partial(kernel, gx, gy),
        out_shape=out_shape,
        in_specs=[main] * 10,
        out_specs=(anywhere,) * 3,
        scratch_shapes=shapes,
        compiler_params=pltpu.CompilerParams(
            collective_id=0, has_side_effects=True, vmem_limit_bytes=64 * 1024 * 1024
        ),
    )(e_field, h_field, inverse_permittivity, monitor_layer, source_layer, residual_far, *consts)
    return pl.pallas_call(
        hand_out,
        out_shape=out_shape,
        in_specs=[anywhere] * 3,
        out_specs=(main,) * 3,
        scratch_shapes=[pltpu.VMEM(shape.shape, f32) for shape in out_shape] + [dma((3 + freqs + 3,))] * 2,
        compiler_params=pltpu.CompilerParams(vmem_limit_bytes=64 * 1024 * 1024),
    )(*results)


def solution(mesh):
    in_specs = (
        P("design", None, "gx", "gy"),
        P("design", None, "gx", "gy"),
        P("design", "gx", "gy"),
        P(("design", "gx"), "gy"),
        P(("design", "gx"), "gy"),
        P("design", None, None, "gx", "gy"),
    )
    out_specs = (
        P("design", None, "gx", "gy"),
        P("design", None, None, "gx", "gy"),
        P("design", None, "gx", "gy"),
    )
    gx, gy = mesh.shape["gx"], mesh.shape["gy"]

    def local(e_field, h_field, inverse_permittivity, monitor_layer, source_layer, residual_far):
        _, _, nx, ny = e_field.shape
        na, nb = residual_far.shape[3:]
        consts = [jnp.asarray(table) for table in tables(gx, gy, na, nb, nx, ny)]
        return per_device(consts, gx, gy, e_field, h_field, inverse_permittivity, monitor_layer,
                          source_layer, residual_far)

    return jax.shard_map(local, mesh=mesh, in_specs=in_specs, out_specs=out_specs, check_vma=False)
```

```python
import functools
import math

import jax
import jax.numpy as jnp
import numpy as np
from jax import lax
from jax.experimental import pallas as pl
from jax.experimental.pallas import tpu as pltpu
from jax.sharding import PartitionSpec as P

courant = 0.5
omegas = (0.7, 1.3)
factors = (3, 5)
MESH = pl.DeviceIdType.MESH
ticks = (1, 2)


def angles(dirs, length):
    rows = np.arange(dirs)[:, None] - dirs // 2
    cols = np.arange(length)[None, :]
    return np.stack(
        [np.mod(rows * cols * factor, 4 * length) * (2.0 * np.pi / (4 * length)) for factor in factors]
    )


def tables(gx, gy, na, nb, nx, ny):
    theta = angles(gx * na, gx * nx)
    phi = angles(gy * nb, gy * ny)
    freqs = len(factors)
    shifted = np.stack([phi + np.array(omegas)[:, None, None] * t for t in ticks])
    both = np.stack([np.cos(shifted), -np.sin(shifted)], axis=2)
    both = both.reshape(len(ticks), freqs, 2, gy, nb, gy, ny)
    far_y = both.transpose(3, 0, 5, 6, 1, 2, 4).reshape(gy, len(ticks), gy, ny, freqs * 2 * nb)
    back_y = both.transpose(5, 3, 1, 2, 4, 0, 6).reshape(gy, gy, freqs, 2 * nb, len(ticks) * ny)
    back_y = back_y / (gx * na)
    pair = np.stack([np.cos(theta), np.sin(theta)], axis=1).reshape(freqs, 2, gx, na, gx * nx)
    far_x = pair.transpose(2, 0, 1, 3, 4).reshape(gx, freqs, 2 * na, gx * nx)
    far_x = far_x / math.sqrt(gx * nx * gy * ny)
    cos, sin = np.cos(theta), np.sin(theta)
    mix = np.stack([np.stack([cos, -sin]), np.stack([sin, cos])])
    mix = mix.reshape(2, 2, freqs, gx, na, gx, nx)
    back_x = mix.transpose(3, 2, 5, 0, 6, 1, 4).reshape(gx, freqs, gx * 2 * nx, 2 * na)
    return [table.astype(np.float32) for table in (far_y, back_y, far_x, back_x)]


def split(value):
    high = value.astype(jnp.bfloat16)
    return high, (value - high.astype(jnp.float32)).astype(jnp.bfloat16)


def mul(left, right):
    return jnp.dot(left, right, preferred_element_type=jnp.float32)


def triple(left, right):
    return mul(left[0], right[0]) + (mul(left[0], right[1]) + mul(left[1], right[0]))


def kernel(
    gx, gy,
    e_in, h_in, k_in, mon_in, src_in, res_in, far_y_in, back_y_in, far_x_in, back_x_in,
    e_out, far_out, adj_out,
    elec, magn, inv, mon, src, res, far_y32, back_y32, far_x, back_x, far_y, back_y,
    aelec, amagn, afinal, far,
    row_send, col_send, row_recv, col_recv, back_rows, back_cols, took_rows, took_cols, corner_row, corner_col,
    vsend, vrecv, vall, planes, qall,
    in_sems, out_sems, halo_send, halo_recv, v_send, v_recv, g_send, g_recv, p_send, p_recv, q_send, q_recv,
):
    mx = lax.axis_index("gx")
    my = lax.axis_index("gy")
    _, nz, nx, ny = e_in.shape
    na, nb = res_in.shape[3:]
    freqs = len(factors)

    loads = {}
    for slot, (name, source, target) in enumerate((
        ("res", res_in, res),
        ("back_x", back_x_in.at[mx], back_x),
        ("e", e_in, elec.at[:, pl.ds(0, nz)]),
        ("h", h_in, magn.at[:, pl.ds(1, nz)]),
        ("k", k_in, inv),
        ("mon", mon_in, mon),
        ("src", src_in, src),
        ("back_y", back_y_in.at[my], back_y32),
        ("far_y", far_y_in.at[my], far_y32),
        ("far_x", far_x_in.at[mx], far_x),
    )):
        loads[name] = pltpu.make_async_copy(source, target, in_sems.at[slot])
        loads[name].start()

    row_recv[...] = jnp.zeros_like(row_recv)
    col_recv[...] = jnp.zeros_like(col_recv)
    for ref in (took_rows, took_cols, corner_row, corner_col):
        ref[...] = jnp.zeros_like(ref)
    blank = jnp.zeros((nx, ny), jnp.float32)
    for part in range(3):
        elec[part, nz] = blank
        magn[part, 0] = blank
        amagn[part, 0] = blank
    for part in range(2):
        aelec[part, nz] = blank

    barrier = pltpu.get_barrier_semaphore()
    for step in range(1, gx):
        pl.semaphore_signal(barrier, inc=1, device_id={"gx": lax.rem(mx + step, gx)}, device_id_type=MESH)
    for step in range(1, gy):
        pl.semaphore_signal(barrier, inc=1, device_id={"gy": lax.rem(my + step, gy)}, device_id_type=MESH)

    has_fore = (mx < gx - 1) & (my >= 1)
    has_aft = (mx >= 1) & (my < gy - 1)
    fore = {"gx": lax.rem(mx + 1, gx), "gy": lax.rem(my + gy - 1, gy)}
    aft = {"gx": lax.rem(mx + gx - 1, gx), "gy": lax.rem(my + 1, gy)}

    for diagonal in (fore, aft):
        pl.semaphore_signal(barrier, inc=1, device_id=diagonal, device_id_type=MESH)

    lanes = lax.broadcasted_iota(jnp.int32, (nx, ny), 1)
    rows = lax.broadcasted_iota(jnp.int32, (nx, ny), 0)

    def each_z(body, init):
        return lax.fori_loop(0, nz, body, init, unroll=True)

    def ahead_x(value, edge):
        return jnp.where(rows == nx - 1, edge, pltpu.roll(value, nx - 1, axis=0))

    def behind_x(value, edge):
        return jnp.where(rows == 0, edge, pltpu.roll(value, 1, axis=0))

    def ahead_y(value, packed, lane):
        edge = pltpu.roll(packed, lax.rem(2 * ny - 1 - lane, ny), axis=1)
        return jnp.where(lanes == ny - 1, edge, pltpu.roll(value, ny - 1, axis=1))

    def behind_y(value, packed, lane):
        edge = pltpu.roll(packed, lax.rem(2 * ny - lane, ny), axis=1)
        return jnp.where(lanes == 0, edge, pltpu.roll(value, 1, axis=1))

    def pack_first(value, lane, packed):
        return jnp.where(lanes == lane, pltpu.roll(value, lane, axis=1), packed)

    def pack_last(value, lane, packed):
        return jnp.where(lanes == lane, pltpu.roll(value, lane + 1, axis=1), packed)

    def halo(number, direction, count):
        size = gx, gy
        place = mx, my
        out = []
        for which, (axis, send, recv) in enumerate((("gx", row_send, row_recv), ("gy", col_send, col_recv))):
            here, total = place[which], size[which]
            target = lax.rem(here + direction + total, total)
            source_ref = send.at[number, pl.ds(0, count)] if which == 0 else send.at[number]
            target_ref = recv.at[number, pl.ds(0, count)] if which == 0 else recv.at[number]
            copy = pltpu.make_async_remote_copy(
                src_ref=source_ref,
                dst_ref=target_ref,
                send_sem=halo_send.at[number, which],
                recv_sem=halo_recv.at[number, which],
                device_id={axis: target},
                device_id_type=MESH,
            )
            sends = here >= 1 if direction < 0 else here < total - 1
            takes = here < total - 1 if direction < 0 else here >= 1
            out.append((copy, sends, takes))
        return out

    def wide(number):
        step = number // 2
        out = []
        for which, source, target, device, sends, takes in (
            (2, back_rows.at[step], took_rows.at[step], {"gx": lax.rem(mx + 1, gx)}, mx < gx - 1, mx >= 1),
            (3, back_cols.at[step], took_cols.at[step], {"gy": lax.rem(my + 1, gy)}, my < gy - 1, my >= 1),
            (4, back_rows.at[step, 2], corner_row.at[step], fore, has_fore, has_aft),
            (5, back_cols.at[step], corner_col.at[step], aft, has_aft, has_fore),
        ):
            out.append((pltpu.make_async_remote_copy(
                src_ref=source, dst_ref=target,
                send_sem=halo_send.at[number, which], recv_sem=halo_recv.at[number, which],
                device_id=device, device_id_type=MESH), sends, takes))
        return out

    halos = {number: halo(number, direction, count) for number, direction, count in (
        (0, -1, 2), (2, -1, 2), (4, -1, 1), (5, 1, 2))}
    for number in (0, 2):
        halos[number] += wide(number)

    def send_halo(number):
        for copy, sends, _ in halos[number]:
            pl.when(sends)(copy.start)

    def take_halo(number):
        for copy, _, takes in halos[number]:
            pl.when(takes)(copy.wait_recv)

    def end_halo(number):
        for copy, sends, _ in halos[number]:
            pl.when(sends)(copy.wait_send)

    def spread(axis, source, target, send, recv):
        here, total = (mx, gx) if axis == "gx" else (my, gy)
        out = []
        for step in range(1, total):
            other = lax.rem(here + step, total)
            out.append((
                pltpu.make_async_remote_copy(
                    src_ref=source(other), dst_ref=target(here),
                    send_sem=send(other), recv_sem=recv(here),
                    device_id={axis: other}, device_id_type=MESH),
                pltpu.make_async_remote_copy(
                    src_ref=source(other), dst_ref=target(other),
                    send_sem=send(other), recv_sem=recv(other),
                    device_id={axis: other}, device_id_type=MESH),
            ))
        return out

    def start(copies):
        for copy, _ in copies:
            copy.start()

    def arrive(copies):
        for _, copy in copies:
            copy.wait_recv()

    def left(copies):
        for copy, _ in copies:
            copy.wait_send()

    loads["res"].wait()
    loads["back_x"].wait()
    for f in range(freqs):
        block = jnp.concatenate(
            [jnp.concatenate([res[f, c, 0], res[f, c, 1]], axis=0) for c in range(2)], axis=1)
        part = triple(split(back_x[f]), split(block))
        for other in range(gx):
            vsend[other, f] = part[other * 2 * nx:(other + 1) * 2 * nx]

    loads["e"].wait()

    loads["h"].wait()

    def pack_start(z, carry):
        first, last = carry
        ex, ey, ez = elec[0, z], elec[1, z], elec[2, z]
        hx, hy, hz = magn[0, z + 1], magn[1, z + 1], magn[2, z + 1]
        row_send[0, 0, pl.ds(z, 1)] = ey[0:1]
        row_send[0, 1, pl.ds(z, 1)] = ez[0:1]
        first = pack_first(ez, nz + z, pack_first(ex, z, first))
        for slot, value in enumerate((hy, hz, ex, ey, ez)):
            back_rows[0, slot, pl.ds(z, 1)] = value[nx - 1:nx]
        for slot, value in enumerate((hx, hz, ex, ey, ez)):
            last = pack_last(value, slot * nz + z, last)
        return first, last

    col_send[0], back_cols[0] = each_z(pack_start, (blank, blank))
    pl.semaphore_wait(barrier, gx + gy)

    send_halo(0)
    v_copies = spread("gx", lambda other: vsend.at[other], lambda slot: vrecv.at[slot],
                      lambda other: v_send.at[other], lambda slot: v_recv.at[slot])
    start(v_copies)

    loads["back_y"].wait()
    for slot in range(gy):
        for f in range(freqs):
            back_y[slot, f, 0], back_y[slot, f, 1] = split(back_y32[slot, f])
    loads["far_y"].wait()
    for tick in range(len(ticks)):
        for slot in range(gy):
            far_y[tick, slot, 0], far_y[tick, slot, 1] = split(far_y32[tick, slot])

    zrows = lax.broadcasted_iota(jnp.int32, (nz, ny), 0)

    def left_by(value, count):
        return pltpu.roll(value, (2 * ny - count) % ny, axis=1)

    def borders(number):
        step = number // 2
        hy, hz, ex, ey, ez = [took_rows[step, slot] for slot in range(5)]
        up = jnp.where(zrows == nz - 1, 0.0, pltpu.roll(ex, nz - 1, axis=0))
        hy = hy - courant * ((up - ex) - (row_send[number, 1] - ez))
        side = jnp.where(jnp.broadcast_to(lanes[0:1], (nz, ny)) == ny - 1,
                         pltpu.roll(corner_row[step], ny - 1, axis=1), pltpu.roll(ex, ny - 1, axis=1))
        hz = hz - courant * ((row_send[number, 0] - ey) - (side - ex))
        row_recv[number + 1, 0] = jnp.where(mx >= 1, hy, 0.0)
        row_recv[number + 1, 1] = jnp.where(mx >= 1, hz, 0.0)
        took, mine = took_cols[step], col_send[number]
        ey = left_by(took, 3 * nz)
        up = jnp.where(lanes == nz - 1, 0.0, left_by(took, 3 * nz + 1))
        hx = took - courant * ((left_by(mine, nz) - left_by(took, 4 * nz)) - (up - ey))
        side = ahead_x(took, pltpu.roll(corner_col[step], nx - 1, axis=0))
        hz = took - courant * ((left_by(side, 2 * nz) - left_by(took, 2 * nz))
                               - (left_by(mine, ny - nz) - left_by(took, nz)))
        col_recv[number + 1] = jnp.where(my >= 1, jnp.where(lanes < nz, hx, hz), 0.0)

    def magnetic(number, wider):
        def body(z, packed):
            ex, ey, ez = elec[0, z], elec[1, z], elec[2, z]
            x_face = row_recv.at[number]
            next_x1 = ahead_x(ey, x_face[0, pl.ds(z, 1)])
            next_x2 = ahead_x(ez, x_face[1, pl.ds(z, 1)])
            cols = col_recv[number]
            next_y0 = ahead_y(ex, cols, z)
            next_y2 = ahead_y(ez, cols, nz + z)
            hx = magn[0, z + 1] - courant * ((next_y2 - ez) - (elec[1, z + 1] - ey))
            hy = magn[1, z + 1] - courant * ((elec[0, z + 1] - ex) - (next_x2 - ez))
            hz = magn[2, z + 1] - courant * ((next_x1 - ey) - (next_y0 - ex))
            magn[0, z + 1] = hx
            magn[1, z + 1] = hy
            magn[2, z + 1] = hz
            if wider:
                back_rows[1, 0, pl.ds(z, 1)] = hy[nx - 1:nx]
                back_rows[1, 1, pl.ds(z, 1)] = hz[nx - 1:nx]
                packed = pack_last(hz, nz + z, pack_last(hx, z, packed))
            return packed
        packed = each_z(body, blank)
        if wider:
            back_cols[1] = packed

    def curls(field, number, z):
        hx, hy, hz = field[0, z + 1], field[1, z + 1], field[2, z + 1]
        x_face = row_recv.at[number]
        prev_x1 = behind_x(hy, x_face[0, pl.ds(z, 1)])
        prev_x2 = behind_x(hz, x_face[1, pl.ds(z, 1)])
        cols = col_recv[number]
        prev_y0 = behind_y(hx, cols, z)
        prev_y2 = behind_y(hz, cols, nz + z)
        curl_x = (hz - prev_y2) - (hy - field[1, z])
        curl_y = (hx - field[0, z]) - (hz - prev_x2)
        curl_z = (hy - prev_x1) - (hx - prev_y0)
        return curl_x, curl_y, curl_z

    def electric(number, after, tick):
        def body(z, carry):
            packed, last, plane_x, plane_y = carry
            gain = courant * inv[z]
            curl_x, curl_y, curl_z = curls(magn, number, z)
            ex = elec[0, z] + gain * curl_x
            ey = elec[1, z] + gain * curl_y
            ez = elec[2, z] + gain * curl_z
            elec[0, z] = ex
            elec[1, z] = ey
            elec[2, z] = ez
            seen = mon[...] == z
            plane_x = jnp.where(seen, ex, plane_x)
            plane_y = jnp.where(seen, ey, plane_y)
            if after is not None:
                row_send[after, 0, pl.ds(z, 1)] = ey[0:1]
                row_send[after, 1, pl.ds(z, 1)] = ez[0:1]
                packed = pack_first(ez, nz + z, pack_first(ex, z, packed))
                for slot, value in ((2, ex), (3, ey), (4, ez)):
                    back_rows[1, slot, pl.ds(z, 1)] = value[nx - 1:nx]
                    last = pack_last(value, slot * nz + z, last)
            return packed, last, plane_x, plane_y
        packed, last, plane_x, plane_y = each_z(body, (blank, back_cols[1], blank, blank))
        if after is not None:
            col_send[after] = packed
            back_cols[1] = last
        planes[tick, my, 0:nx] = plane_x
        planes[tick, my, nx:2 * nx] = plane_y

    def plane_copies(tick):
        return spread("gy", lambda other: planes.at[tick, my], lambda slot: planes.at[tick, slot],
                      lambda other: p_send.at[tick, other], lambda slot: p_recv.at[tick, slot])

    first_planes, second_planes = plane_copies(0), plane_copies(1)
    g_copies = spread("gy", lambda other: vall.at[my], lambda slot: vall.at[slot],
                      lambda other: g_send.at[other], lambda slot: g_recv.at[slot])
    q_copies = spread("gx", lambda other: qall.at[:, mx], lambda slot: qall.at[:, slot],
                      lambda other: q_send.at[other], lambda slot: q_recv.at[slot])

    take_halo(0)
    borders(0)

    arrive(v_copies)
    vrecv[mx] = vsend[mx]
    for f in range(freqs):
        total = vrecv[0, f]
        for slot in range(1, gx):
            total = total + vrecv[slot, f]
        top, low = total[0:nx], total[nx:2 * nx]
        for c in range(2):
            vall[my, f, c * nx:(c + 1) * nx] = jnp.concatenate(
                [top[:, c * nb:(c + 1) * nb], low[:, c * nb:(c + 1) * nb]], axis=1)
    start(g_copies)

    for name in ("k", "mon", "src"):
        loads[name].wait()
    magnetic(0, True)
    electric(1, 2, 0)
    send_halo(2)
    start(first_planes)

    arrive(g_copies)
    drive = jnp.zeros((2 * nx, len(ticks) * ny), jnp.float32)
    for slot in range(gy):
        for f in range(freqs):
            drive = drive + triple(split(vall[slot, f]), (back_y[slot, f, 0], back_y[slot, f, 1]))

    def adjoint_first(z, packed):
        lit = jnp.where(src[...] == z, (-courant) * inv[z], 0.0)
        ex = lit * drive[0:nx, 0:ny]
        ey = lit * drive[nx:2 * nx, 0:ny]
        aelec[0, z] = ex
        aelec[1, z] = ey
        row_send[4, 0, pl.ds(z, 1)] = ey[0:1]
        return pack_first(ex, z, packed)

    col_send[4] = each_z(adjoint_first, blank)
    send_halo(4)

    take_halo(2)
    borders(2)
    magnetic(2, False)
    electric(3, None, 1)
    start(second_planes)
    stores = [pltpu.make_async_copy(elec.at[:, pl.ds(0, nz)], e_out, out_sems.at[0])]
    stores[0].start()

    take_halo(4)

    def adjoint_magnetic(z, packed):
        ex, ey = aelec[0, z], aelec[1, z]
        next_x1 = ahead_x(ey, row_recv[4, 0, pl.ds(z, 1)])
        next_y0 = ahead_y(ex, col_recv[4], z)
        hx = courant * (aelec[1, z + 1] - ey)
        hy = (-courant) * (aelec[0, z + 1] - ex)
        hz = (-courant) * ((next_x1 - ey) - (next_y0 - ex))
        amagn[0, z + 1] = hx
        amagn[1, z + 1] = hy
        amagn[2, z + 1] = hz
        row_send[5, 0, pl.ds(z, 1)] = hy[nx - 1:nx]
        row_send[5, 1, pl.ds(z, 1)] = hz[nx - 1:nx]
        return pack_last(hz, nz + z, pack_last(hx, z, packed))

    col_send[5] = each_z(adjoint_magnetic, blank)
    send_halo(5)

    def project(tick):
        total = 0.0
        for slot in range(gy):
            total = total + triple(split(planes[tick, slot]), (far_y[tick, slot, 0], far_y[tick, slot, 1]))
        return total

    arrive(first_planes)
    early = project(0)
    arrive(second_planes)
    half = early + project(1)
    for c in range(2):
        qall[c, mx] = half[c * nx:(c + 1) * nx]
    start(q_copies)

    take_halo(5)

    def adjoint_second(z, carry):
        gain = courant * inv[z]
        curl_x, curl_y, curl_z = curls(amagn, 5, z)
        lit = src[...] == z
        afinal[0, z] = aelec[0, z] + gain * (curl_x - jnp.where(lit, drive[0:nx, ny:2 * ny], 0.0))
        afinal[1, z] = aelec[1, z] + gain * (curl_y - jnp.where(lit, drive[nx:2 * nx, ny:2 * ny], 0.0))
        afinal[2, z] = gain * curl_z
        return carry

    each_z(adjoint_second, 0)
    stores.append(pltpu.make_async_copy(afinal, adj_out, out_sems.at[1]))
    stores[1].start()

    loads["far_x"].wait()
    arrive(q_copies)
    for c in range(2):
        high, low = split(jnp.reshape(qall[c], (gx * nx, freqs * 2 * nb)))
        for f in range(freqs):
            cut = slice(f * 2 * nb, (f + 1) * 2 * nb)
            both = triple(split(far_x[f]), (high[:, cut], low[:, cut]))
            far[f, c, 0] = both[0:na, 0:nb] + both[na:2 * na, nb:2 * nb]
            far[f, c, 1] = both[0:na, nb:2 * nb] - both[na:2 * na, 0:nb]
    stores.append(pltpu.make_async_copy(far, far_out, out_sems.at[2]))
    stores[2].start()

    for number in (0, 2, 4, 5):
        end_halo(number)
    for copies in (v_copies, g_copies, first_planes, second_planes, q_copies):
        left(copies)
    for copy in stores:
        copy.wait()


def hand_out(e_made, far_made, adj_made, e_out, far_out, adj_out, e_held, far_held, adj_held, load_sems, store_sems):
    moves = []
    for made, held, out in ((e_made, e_held, e_out), (far_made, far_held, far_out), (adj_made, adj_held, adj_out)):
        for part in range(made.shape[0]):
            slot = len(moves)
            moves.append((
                pltpu.make_async_copy(made.at[part], held.at[part], load_sems.at[slot]),
                pltpu.make_async_copy(held.at[part], out.at[part], store_sems.at[slot]),
            ))
    for load, _ in moves:
        load.start()
    for load, store in moves:
        load.wait()
        store.start()
    for _, store in moves:
        store.wait()


def per_device(consts, gx, gy, e_field, h_field, inverse_permittivity, monitor_layer, source_layer, residual_far):
    _, nz, nx, ny = e_field.shape
    freqs = len(factors)
    na, nb = residual_far.shape[3:]
    f32 = jnp.float32
    shapes = [
        pltpu.VMEM((3, nz + 1, nx, ny), f32),
        pltpu.VMEM((3, nz + 1, nx, ny), f32),
        pltpu.VMEM(inverse_permittivity.shape, f32),
        pltpu.VMEM(monitor_layer.shape, jnp.int32),
        pltpu.VMEM(source_layer.shape, jnp.int32),
        pltpu.VMEM(residual_far.shape, f32),
    ] + [pltpu.VMEM(const.shape[1:], f32) for const in consts] + [
        pltpu.VMEM(const.shape[1:-2] + (2,) + const.shape[-2:], jnp.bfloat16) for const in consts[:2]
    ] + [
        pltpu.VMEM((2, nz + 1, nx, ny), f32),
        pltpu.VMEM((3, nz + 1, nx, ny), f32),
        pltpu.VMEM((3, nz, nx, ny), f32),
        pltpu.VMEM(residual_far.shape, f32),
        pltpu.VMEM((6, 2, nz, ny), f32),
        pltpu.VMEM((6, nx, ny), f32),
        pltpu.VMEM((6, 2, nz, ny), f32),
        pltpu.VMEM((6, nx, ny), f32),
        pltpu.VMEM((2, 5, nz, ny), f32),
        pltpu.VMEM((2, nx, ny), f32),
        pltpu.VMEM((2, 5, nz, ny), f32),
        pltpu.VMEM((2, nx, ny), f32),
        pltpu.VMEM((2, nz, ny), f32),
        pltpu.VMEM((2, nx, ny), f32),
        pltpu.VMEM((gx, freqs, 2 * nx, 2 * nb), f32),
        pltpu.VMEM((gx, freqs, 2 * nx, 2 * nb), f32),
        pltpu.VMEM((gy, freqs, 2 * nx, 2 * nb), f32),
        pltpu.VMEM((len(ticks), gy, 2 * nx, ny), f32),
        pltpu.VMEM((2, gx, nx, freqs * 2 * nb), f32),
    ]
    dma = pltpu.SemaphoreType.DMA
    shapes += [dma((10,)), dma((3,)), dma((6, 6)), dma((6, 6)), dma((gx,)), dma((gx,)), dma((gy,)), dma((gy,)),
               dma((len(ticks), gy)), dma((len(ticks), gy)), dma((gx,)), dma((gx,))]
    anywhere = pl.BlockSpec(memory_space=pl.ANY)
    main = pl.BlockSpec(memory_space=pltpu.HBM)
    out_shape = (
        jax.ShapeDtypeStruct(e_field.shape, f32),
        jax.ShapeDtypeStruct(residual_far.shape, f32),
        jax.ShapeDtypeStruct(e_field.shape, f32),
    )
    results = pl.pallas_call(
        functools.partial(kernel, gx, gy),
        out_shape=out_shape,
        in_specs=[main] * 10,
        out_specs=(anywhere,) * 3,
        scratch_shapes=shapes,
        compiler_params=pltpu.CompilerParams(
            collective_id=0, has_side_effects=True, vmem_limit_bytes=64 * 1024 * 1024
        ),
    )(e_field, h_field, inverse_permittivity, monitor_layer, source_layer, residual_far, *consts)
    return pl.pallas_call(
        hand_out,
        out_shape=out_shape,
        in_specs=[anywhere] * 3,
        out_specs=(main,) * 3,
        scratch_shapes=[pltpu.VMEM(shape.shape, f32) for shape in out_shape] + [dma((3 + freqs + 3,))] * 2,
        compiler_params=pltpu.CompilerParams(vmem_limit_bytes=64 * 1024 * 1024),
    )(*results)


def solution(mesh):
    in_specs = (
        P("design", None, "gx", "gy"),
        P("design", None, "gx", "gy"),
        P("design", "gx", "gy"),
        P(("design", "gx"), "gy"),
        P(("design", "gx"), "gy"),
        P("design", None, None, "gx", "gy"),
    )
    out_specs = (
        P("design", None, "gx", "gy"),
        P("design", None, None, "gx", "gy"),
        P("design", None, "gx", "gy"),
    )
    gx, gy = mesh.shape["gx"], mesh.shape["gy"]

    def local(e_field, h_field, inverse_permittivity, monitor_layer, source_layer, residual_far):
        _, _, nx, ny = e_field.shape
        na, nb = residual_far.shape[3:]
        consts = [jnp.asarray(table) for table in tables(gx, gy, na, nb, nx, ny)]
        return per_device(consts, gx, gy, e_field, h_field, inverse_permittivity, monitor_layer,
                          source_layer, residual_far)

    return jax.shard_map(local, mesh=mesh, in_specs=in_specs, out_specs=out_specs, check_vma=False)
```

```python
import functools
import math

import jax
import jax.numpy as jnp
import numpy as np
from jax import lax
from jax.experimental import pallas as pl
from jax.experimental.pallas import tpu as pltpu
from jax.sharding import PartitionSpec as P

courant = 0.5
omegas = (0.7, 1.3)
factors = (3, 5)
MESH = pl.DeviceIdType.MESH
ticks = (1, 2)


def angles(dirs, length):
    rows = np.arange(dirs)[:, None] - dirs // 2
    cols = np.arange(length)[None, :]
    return np.stack(
        [np.mod(rows * cols * factor, 4 * length) * (2.0 * np.pi / (4 * length)) for factor in factors]
    )


def tables(gx, gy, na, nb, nx, ny):
    theta = angles(gx * na, gx * nx)
    phi = angles(gy * nb, gy * ny)
    freqs = len(factors)
    shifted = np.stack([phi + np.array(omegas)[:, None, None] * t for t in ticks])
    both = np.stack([np.cos(shifted), -np.sin(shifted)], axis=2)
    both = both.reshape(len(ticks), freqs, 2, gy, nb, gy, ny)
    far_y = both.transpose(3, 0, 5, 6, 1, 2, 4).reshape(gy, len(ticks), gy, ny, freqs * 2 * nb)
    back_y = both.transpose(5, 3, 1, 2, 4, 0, 6).reshape(gy, gy, freqs, 2 * nb, len(ticks) * ny)
    back_y = back_y / (gx * na)
    pair = np.stack([np.cos(theta), np.sin(theta)], axis=1).reshape(freqs, 2, gx, na, gx * nx)
    far_x = pair.transpose(2, 0, 1, 3, 4).reshape(gx, freqs, 2 * na, gx * nx)
    far_x = far_x / math.sqrt(gx * nx * gy * ny)
    cos, sin = np.cos(theta), np.sin(theta)
    mix = np.stack([np.stack([cos, -sin]), np.stack([sin, cos])])
    mix = mix.reshape(2, 2, freqs, gx, na, gx, nx)
    back_x = mix.transpose(3, 2, 5, 0, 6, 1, 4).reshape(gx, freqs, gx * 2 * nx, 2 * na)
    return [table.astype(np.float32) for table in (far_y, back_y, far_x, back_x)]


def split(value):
    high = value.astype(jnp.bfloat16)
    return high, (value - high.astype(jnp.float32)).astype(jnp.bfloat16)


def mul(left, right):
    return jnp.dot(left, right, preferred_element_type=jnp.float32)


def triple(left, right):
    return mul(left[0], right[0]) + (mul(left[0], right[1]) + mul(left[1], right[0]))


def kernel(
    gx, gy,
    e_in, h_in, k_in, mon_in, src_in, res_in, far_y_in, back_y_in, far_x_in, back_x_in,
    e_out, far_out, adj_out,
    elec, magn, inv, mon, src, res, far_y32, back_y32, far_x, back_x, far_y, back_y,
    aelec, amagn, afinal, far,
    row_send, col_send, row_recv, col_recv, back_rows, back_cols, took_rows, took_cols, corner_row, corner_col,
    vsend, vrecv, vall, planes, qall,
    in_sems, out_sems, halo_send, halo_recv, v_send, v_recv, g_send, g_recv, p_send, p_recv, q_send, q_recv,
):
    mx = lax.axis_index("gx")
    my = lax.axis_index("gy")
    _, nz, nx, ny = e_in.shape
    na, nb = res_in.shape[3:]
    freqs = len(factors)

    loads = {}
    for slot, (name, source, target) in enumerate((
        ("e", e_in, elec.at[:, pl.ds(0, nz)]),
        ("h", h_in, magn.at[:, pl.ds(1, nz)]),
        ("res", res_in, res),
        ("back_x", back_x_in.at[mx], back_x),
        ("k", k_in, inv),
        ("mon", mon_in, mon),
        ("src", src_in, src),
        ("back_y", back_y_in.at[my], back_y32),
        ("far_y", far_y_in.at[my], far_y32),
        ("far_x", far_x_in.at[mx], far_x),
    )):
        loads[name] = pltpu.make_async_copy(source, target, in_sems.at[slot])
        loads[name].start()

    row_recv[...] = jnp.zeros_like(row_recv)
    col_recv[...] = jnp.zeros_like(col_recv)
    for ref in (took_rows, took_cols, corner_row, corner_col):
        ref[...] = jnp.zeros_like(ref)
    blank = jnp.zeros((nx, ny), jnp.float32)
    for part in range(3):
        elec[part, nz] = blank
        magn[part, 0] = blank
        amagn[part, 0] = blank
    for part in range(2):
        aelec[part, nz] = blank

    barrier = pltpu.get_barrier_semaphore()
    for step in range(1, gx):
        pl.semaphore_signal(barrier, inc=1, device_id={"gx": lax.rem(mx + step, gx)}, device_id_type=MESH)
    for step in range(1, gy):
        pl.semaphore_signal(barrier, inc=1, device_id={"gy": lax.rem(my + step, gy)}, device_id_type=MESH)

    has_fore = (mx < gx - 1) & (my >= 1)
    has_aft = (mx >= 1) & (my < gy - 1)
    fore = {"gx": lax.rem(mx + 1, gx), "gy": lax.rem(my + gy - 1, gy)}
    aft = {"gx": lax.rem(mx + gx - 1, gx), "gy": lax.rem(my + 1, gy)}

    for diagonal in (fore, aft):
        pl.semaphore_signal(barrier, inc=1, device_id=diagonal, device_id_type=MESH)

    lanes = lax.broadcasted_iota(jnp.int32, (nx, ny), 1)
    rows = lax.broadcasted_iota(jnp.int32, (nx, ny), 0)

    def each_z(body, init):
        return lax.fori_loop(0, nz, body, init, unroll=True)

    def ahead_x(value, edge):
        return jnp.where(rows == nx - 1, edge, pltpu.roll(value, nx - 1, axis=0))

    def behind_x(value, edge):
        return jnp.where(rows == 0, edge, pltpu.roll(value, 1, axis=0))

    def ahead_y(value, packed, lane):
        edge = pltpu.roll(packed, lax.rem(2 * ny - 1 - lane, ny), axis=1)
        return jnp.where(lanes == ny - 1, edge, pltpu.roll(value, ny - 1, axis=1))

    def behind_y(value, packed, lane):
        edge = pltpu.roll(packed, lax.rem(2 * ny - lane, ny), axis=1)
        return jnp.where(lanes == 0, edge, pltpu.roll(value, 1, axis=1))

    def pack_first(value, lane, packed):
        return jnp.where(lanes == lane, pltpu.roll(value, lane, axis=1), packed)

    def pack_last(value, lane, packed):
        return jnp.where(lanes == lane, pltpu.roll(value, lane + 1, axis=1), packed)

    def halo(number, direction, count):
        size = gx, gy
        place = mx, my
        out = []
        for which, (axis, send, recv) in enumerate((("gx", row_send, row_recv), ("gy", col_send, col_recv))):
            here, total = place[which], size[which]
            target = lax.rem(here + direction + total, total)
            source_ref = send.at[number, pl.ds(0, count)] if which == 0 else send.at[number]
            target_ref = recv.at[number, pl.ds(0, count)] if which == 0 else recv.at[number]
            copy = pltpu.make_async_remote_copy(
                src_ref=source_ref,
                dst_ref=target_ref,
                send_sem=halo_send.at[number, which],
                recv_sem=halo_recv.at[number, which],
                device_id={axis: target},
                device_id_type=MESH,
            )
            sends = here >= 1 if direction < 0 else here < total - 1
            takes = here < total - 1 if direction < 0 else here >= 1
            out.append((copy, sends, takes))
        return out

    def wide(number):
        step = number // 2
        out = []
        for which, source, target, device, sends, takes in (
            (2, back_rows.at[step], took_rows.at[step], {"gx": lax.rem(mx + 1, gx)}, mx < gx - 1, mx >= 1),
            (3, back_cols.at[step], took_cols.at[step], {"gy": lax.rem(my + 1, gy)}, my < gy - 1, my >= 1),
            (4, back_rows.at[step, 2], corner_row.at[step], fore, has_fore, has_aft),
            (5, back_cols.at[step], corner_col.at[step], aft, has_aft, has_fore),
        ):
            out.append((pltpu.make_async_remote_copy(
                src_ref=source, dst_ref=target,
                send_sem=halo_send.at[number, which], recv_sem=halo_recv.at[number, which],
                device_id=device, device_id_type=MESH), sends, takes))
        return out

    halos = {number: halo(number, direction, count) for number, direction, count in (
        (0, -1, 2), (2, -1, 2), (4, -1, 1), (5, 1, 2))}
    for number in (0, 2):
        halos[number] += wide(number)

    def send_halo(number):
        for copy, sends, _ in halos[number]:
            pl.when(sends)(copy.start)

    def take_halo(number):
        for copy, _, takes in halos[number]:
            pl.when(takes)(copy.wait_recv)

    def end_halo(number):
        for copy, sends, _ in halos[number]:
            pl.when(sends)(copy.wait_send)

    def spread(axis, source, target, send, recv):
        here, total = (mx, gx) if axis == "gx" else (my, gy)
        out = []
        for step in range(1, total):
            other = lax.rem(here + step, total)
            out.append((
                pltpu.make_async_remote_copy(
                    src_ref=source(other), dst_ref=target(here),
                    send_sem=send(other), recv_sem=recv(here),
                    device_id={axis: other}, device_id_type=MESH),
                pltpu.make_async_remote_copy(
                    src_ref=source(other), dst_ref=target(other),
                    send_sem=send(other), recv_sem=recv(other),
                    device_id={axis: other}, device_id_type=MESH),
            ))
        return out

    def start(copies):
        for copy, _ in copies:
            copy.start()

    def arrive(copies):
        for _, copy in copies:
            copy.wait_recv()

    def left(copies):
        for copy, _ in copies:
            copy.wait_send()

    loads["e"].wait()

    loads["h"].wait()

    def pack_start(z, carry):
        first, last = carry
        ex, ey, ez = elec[0, z], elec[1, z], elec[2, z]
        hx, hy, hz = magn[0, z + 1], magn[1, z + 1], magn[2, z + 1]
        row_send[0, 0, pl.ds(z, 1)] = ey[0:1]
        row_send[0, 1, pl.ds(z, 1)] = ez[0:1]
        first = pack_first(ez, nz + z, pack_first(ex, z, first))
        for slot, value in enumerate((hy, hz, ex, ey, ez)):
            back_rows[0, slot, pl.ds(z, 1)] = value[nx - 1:nx]
        for slot, value in enumerate((hx, hz, ex, ey, ez)):
            last = pack_last(value, slot * nz + z, last)
        return first, last

    col_send[0], back_cols[0] = each_z(pack_start, (blank, blank))
    pl.semaphore_wait(barrier, gx + gy)

    send_halo(0)

    loads["res"].wait()
    loads["back_x"].wait()
    for f in range(freqs):
        block = jnp.concatenate(
            [jnp.concatenate([res[f, c, 0], res[f, c, 1]], axis=0) for c in range(2)], axis=1)
        part = triple(split(back_x[f]), split(block))
        for other in range(gx):
            vsend[other, f] = part[other * 2 * nx:(other + 1) * 2 * nx]

    v_copies = spread("gx", lambda other: vsend.at[other], lambda slot: vrecv.at[slot],
                      lambda other: v_send.at[other], lambda slot: v_recv.at[slot])
    start(v_copies)

    loads["back_y"].wait()
    for slot in range(gy):
        for f in range(freqs):
            back_y[slot, f, 0], back_y[slot, f, 1] = split(back_y32[slot, f])
    loads["far_y"].wait()
    for tick in range(len(ticks)):
        for slot in range(gy):
            far_y[tick, slot, 0], far_y[tick, slot, 1] = split(far_y32[tick, slot])

    zrows = lax.broadcasted_iota(jnp.int32, (nz, ny), 0)

    def left_by(value, count):
        return pltpu.roll(value, (2 * ny - count) % ny, axis=1)

    def borders(number):
        step = number // 2
        hy, hz, ex, ey, ez = [took_rows[step, slot] for slot in range(5)]
        up = jnp.where(zrows == nz - 1, 0.0, pltpu.roll(ex, nz - 1, axis=0))
        hy = hy - courant * ((up - ex) - (row_send[number, 1] - ez))
        side = jnp.where(jnp.broadcast_to(lanes[0:1], (nz, ny)) == ny - 1,
                         pltpu.roll(corner_row[step], ny - 1, axis=1), pltpu.roll(ex, ny - 1, axis=1))
        hz = hz - courant * ((row_send[number, 0] - ey) - (side - ex))
        row_recv[number + 1, 0] = jnp.where(mx >= 1, hy, 0.0)
        row_recv[number + 1, 1] = jnp.where(mx >= 1, hz, 0.0)
        took, mine = took_cols[step], col_send[number]
        ey = left_by(took, 3 * nz)
        up = jnp.where(lanes == nz - 1, 0.0, left_by(took, 3 * nz + 1))
        hx = took - courant * ((left_by(mine, nz) - left_by(took, 4 * nz)) - (up - ey))
        side = ahead_x(took, pltpu.roll(corner_col[step], nx - 1, axis=0))
        hz = took - courant * ((left_by(side, 2 * nz) - left_by(took, 2 * nz))
                               - (left_by(mine, ny - nz) - left_by(took, nz)))
        col_recv[number + 1] = jnp.where(my >= 1, jnp.where(lanes < nz, hx, hz), 0.0)

    def magnetic(number, wider):
        def body(z, packed):
            ex, ey, ez = elec[0, z], elec[1, z], elec[2, z]
            x_face = row_recv.at[number]
            next_x1 = ahead_x(ey, x_face[0, pl.ds(z, 1)])
            next_x2 = ahead_x(ez, x_face[1, pl.ds(z, 1)])
            cols = col_recv[number]
            next_y0 = ahead_y(ex, cols, z)
            next_y2 = ahead_y(ez, cols, nz + z)
            hx = magn[0, z + 1] - courant * ((next_y2 - ez) - (elec[1, z + 1] - ey))
            hy = magn[1, z + 1] - courant * ((elec[0, z + 1] - ex) - (next_x2 - ez))
            hz = magn[2, z + 1] - courant * ((next_x1 - ey) - (next_y0 - ex))
            magn[0, z + 1] = hx
            magn[1, z + 1] = hy
            magn[2, z + 1] = hz
            if wider:
                back_rows[1, 0, pl.ds(z, 1)] = hy[nx - 1:nx]
                back_rows[1, 1, pl.ds(z, 1)] = hz[nx - 1:nx]
                packed = pack_last(hz, nz + z, pack_last(hx, z, packed))
            return packed
        packed = each_z(body, blank)
        if wider:
            back_cols[1] = packed

    def curls(field, number, z):
        hx, hy, hz = field[0, z + 1], field[1, z + 1], field[2, z + 1]
        x_face = row_recv.at[number]
        prev_x1 = behind_x(hy, x_face[0, pl.ds(z, 1)])
        prev_x2 = behind_x(hz, x_face[1, pl.ds(z, 1)])
        cols = col_recv[number]
        prev_y0 = behind_y(hx, cols, z)
        prev_y2 = behind_y(hz, cols, nz + z)
        curl_x = (hz - prev_y2) - (hy - field[1, z])
        curl_y = (hx - field[0, z]) - (hz - prev_x2)
        curl_z = (hy - prev_x1) - (hx - prev_y0)
        return curl_x, curl_y, curl_z

    def electric(number, after, tick):
        def body(z, carry):
            packed, last, plane_x, plane_y = carry
            gain = courant * inv[z]
            curl_x, curl_y, curl_z = curls(magn, number, z)
            ex = elec[0, z] + gain * curl_x
            ey = elec[1, z] + gain * curl_y
            ez = elec[2, z] + gain * curl_z
            elec[0, z] = ex
            elec[1, z] = ey
            elec[2, z] = ez
            seen = mon[...] == z
            plane_x = jnp.where(seen, ex, plane_x)
            plane_y = jnp.where(seen, ey, plane_y)
            if after is not None:
                row_send[after, 0, pl.ds(z, 1)] = ey[0:1]
                row_send[after, 1, pl.ds(z, 1)] = ez[0:1]
                packed = pack_first(ez, nz + z, pack_first(ex, z, packed))
                for slot, value in ((2, ex), (3, ey), (4, ez)):
                    back_rows[1, slot, pl.ds(z, 1)] = value[nx - 1:nx]
                    last = pack_last(value, slot * nz + z, last)
            return packed, last, plane_x, plane_y
        packed, last, plane_x, plane_y = each_z(body, (blank, back_cols[1], blank, blank))
        if after is not None:
            col_send[after] = packed
            back_cols[1] = last
        planes[tick, my, 0:nx] = plane_x
        planes[tick, my, nx:2 * nx] = plane_y

    def plane_copies(tick):
        return spread("gy", lambda other: planes.at[tick, my], lambda slot: planes.at[tick, slot],
                      lambda other: p_send.at[tick, other], lambda slot: p_recv.at[tick, slot])

    first_planes, second_planes = plane_copies(0), plane_copies(1)
    g_copies = spread("gy", lambda other: vall.at[my], lambda slot: vall.at[slot],
                      lambda other: g_send.at[other], lambda slot: g_recv.at[slot])
    q_copies = spread("gx", lambda other: qall.at[:, mx], lambda slot: qall.at[:, slot],
                      lambda other: q_send.at[other], lambda slot: q_recv.at[slot])

    take_halo(0)
    borders(0)

    arrive(v_copies)
    vrecv[mx] = vsend[mx]
    for f in range(freqs):
        total = vrecv[0, f]
        for slot in range(1, gx):
            total = total + vrecv[slot, f]
        top, low = total[0:nx], total[nx:2 * nx]
        for c in range(2):
            vall[my, f, c * nx:(c + 1) * nx] = jnp.concatenate(
                [top[:, c * nb:(c + 1) * nb], low[:, c * nb:(c + 1) * nb]], axis=1)
    start(g_copies)

    for name in ("k", "mon", "src"):
        loads[name].wait()
    magnetic(0, True)
    electric(1, 2, 0)
    send_halo(2)
    start(first_planes)

    arrive(g_copies)
    drive = jnp.zeros((2 * nx, len(ticks) * ny), jnp.float32)
    for slot in range(gy):
        for f in range(freqs):
            drive = drive + triple(split(vall[slot, f]), (back_y[slot, f, 0], back_y[slot, f, 1]))

    def adjoint_first(z, packed):
        lit = jnp.where(src[...] == z, (-courant) * inv[z], 0.0)
        ex = lit * drive[0:nx, 0:ny]
        ey = lit * drive[nx:2 * nx, 0:ny]
        aelec[0, z] = ex
        aelec[1, z] = ey
        row_send[4, 0, pl.ds(z, 1)] = ey[0:1]
        return pack_first(ex, z, packed)

    col_send[4] = each_z(adjoint_first, blank)
    send_halo(4)

    take_halo(2)
    borders(2)
    magnetic(2, False)
    electric(3, None, 1)
    start(second_planes)
    stores = [pltpu.make_async_copy(elec.at[:, pl.ds(0, nz)], e_out, out_sems.at[0])]
    stores[0].start()

    take_halo(4)

    def adjoint_magnetic(z, packed):
        ex, ey = aelec[0, z], aelec[1, z]
        next_x1 = ahead_x(ey, row_recv[4, 0, pl.ds(z, 1)])
        next_y0 = ahead_y(ex, col_recv[4], z)
        hx = courant * (aelec[1, z + 1] - ey)
        hy = (-courant) * (aelec[0, z + 1] - ex)
        hz = (-courant) * ((next_x1 - ey) - (next_y0 - ex))
        amagn[0, z + 1] = hx
        amagn[1, z + 1] = hy
        amagn[2, z + 1] = hz
        row_send[5, 0, pl.ds(z, 1)] = hy[nx - 1:nx]
        row_send[5, 1, pl.ds(z, 1)] = hz[nx - 1:nx]
        return pack_last(hz, nz + z, pack_last(hx, z, packed))

    col_send[5] = each_z(adjoint_magnetic, blank)
    send_halo(5)

    def project(tick):
        total = 0.0
        for slot in range(gy):
            total = total + triple(split(planes[tick, slot]), (far_y[tick, slot, 0], far_y[tick, slot, 1]))
        return total

    arrive(first_planes)
    early = project(0)
    arrive(second_planes)
    half = early + project(1)
    for c in range(2):
        qall[c, mx] = half[c * nx:(c + 1) * nx]
    start(q_copies)

    take_halo(5)

    def adjoint_second(z, carry):
        gain = courant * inv[z]
        curl_x, curl_y, curl_z = curls(amagn, 5, z)
        lit = src[...] == z
        afinal[0, z] = aelec[0, z] + gain * (curl_x - jnp.where(lit, drive[0:nx, ny:2 * ny], 0.0))
        afinal[1, z] = aelec[1, z] + gain * (curl_y - jnp.where(lit, drive[nx:2 * nx, ny:2 * ny], 0.0))
        afinal[2, z] = gain * curl_z
        return carry

    each_z(adjoint_second, 0)
    stores.append(pltpu.make_async_copy(afinal, adj_out, out_sems.at[1]))
    stores[1].start()

    loads["far_x"].wait()
    arrive(q_copies)
    for c in range(2):
        high, low = split(jnp.reshape(qall[c], (gx * nx, freqs * 2 * nb)))
        for f in range(freqs):
            cut = slice(f * 2 * nb, (f + 1) * 2 * nb)
            both = triple(split(far_x[f]), (high[:, cut], low[:, cut]))
            far[f, c, 0] = both[0:na, 0:nb] + both[na:2 * na, nb:2 * nb]
            far[f, c, 1] = both[0:na, nb:2 * nb] - both[na:2 * na, 0:nb]
    stores.append(pltpu.make_async_copy(far, far_out, out_sems.at[2]))
    stores[2].start()

    for number in (0, 2, 4, 5):
        end_halo(number)
    for copies in (v_copies, g_copies, first_planes, second_planes, q_copies):
        left(copies)
    for copy in stores:
        copy.wait()


def hand_out(e_made, far_made, adj_made, e_out, far_out, adj_out, e_held, far_held, adj_held, load_sems, store_sems):
    moves = []
    for made, held, out in ((e_made, e_held, e_out), (far_made, far_held, far_out), (adj_made, adj_held, adj_out)):
        for part in range(made.shape[0]):
            slot = len(moves)
            moves.append((
                pltpu.make_async_copy(made.at[part], held.at[part], load_sems.at[slot]),
                pltpu.make_async_copy(held.at[part], out.at[part], store_sems.at[slot]),
            ))
    for load, _ in moves:
        load.start()
    for load, store in moves:
        load.wait()
        store.start()
    for _, store in moves:
        store.wait()


def per_device(consts, gx, gy, e_field, h_field, inverse_permittivity, monitor_layer, source_layer, residual_far):
    _, nz, nx, ny = e_field.shape
    freqs = len(factors)
    na, nb = residual_far.shape[3:]
    f32 = jnp.float32
    shapes = [
        pltpu.VMEM((3, nz + 1, nx, ny), f32),
        pltpu.VMEM((3, nz + 1, nx, ny), f32),
        pltpu.VMEM(inverse_permittivity.shape, f32),
        pltpu.VMEM(monitor_layer.shape, jnp.int32),
        pltpu.VMEM(source_layer.shape, jnp.int32),
        pltpu.VMEM(residual_far.shape, f32),
    ] + [pltpu.VMEM(const.shape[1:], f32) for const in consts] + [
        pltpu.VMEM(const.shape[1:-2] + (2,) + const.shape[-2:], jnp.bfloat16) for const in consts[:2]
    ] + [
        pltpu.VMEM((2, nz + 1, nx, ny), f32),
        pltpu.VMEM((3, nz + 1, nx, ny), f32),
        pltpu.VMEM((3, nz, nx, ny), f32),
        pltpu.VMEM(residual_far.shape, f32),
        pltpu.VMEM((6, 2, nz, ny), f32),
        pltpu.VMEM((6, nx, ny), f32),
        pltpu.VMEM((6, 2, nz, ny), f32),
        pltpu.VMEM((6, nx, ny), f32),
        pltpu.VMEM((2, 5, nz, ny), f32),
        pltpu.VMEM((2, nx, ny), f32),
        pltpu.VMEM((2, 5, nz, ny), f32),
        pltpu.VMEM((2, nx, ny), f32),
        pltpu.VMEM((2, nz, ny), f32),
        pltpu.VMEM((2, nx, ny), f32),
        pltpu.VMEM((gx, freqs, 2 * nx, 2 * nb), f32),
        pltpu.VMEM((gx, freqs, 2 * nx, 2 * nb), f32),
        pltpu.VMEM((gy, freqs, 2 * nx, 2 * nb), f32),
        pltpu.VMEM((len(ticks), gy, 2 * nx, ny), f32),
        pltpu.VMEM((2, gx, nx, freqs * 2 * nb), f32),
    ]
    dma = pltpu.SemaphoreType.DMA
    shapes += [dma((10,)), dma((3,)), dma((6, 6)), dma((6, 6)), dma((gx,)), dma((gx,)), dma((gy,)), dma((gy,)),
               dma((len(ticks), gy)), dma((len(ticks), gy)), dma((gx,)), dma((gx,))]
    anywhere = pl.BlockSpec(memory_space=pl.ANY)
    main = pl.BlockSpec(memory_space=pltpu.HBM)
    out_shape = (
        jax.ShapeDtypeStruct(e_field.shape, f32),
        jax.ShapeDtypeStruct(residual_far.shape, f32),
        jax.ShapeDtypeStruct(e_field.shape, f32),
    )
    results = pl.pallas_call(
        functools.partial(kernel, gx, gy),
        out_shape=out_shape,
        in_specs=[main] * 10,
        out_specs=(anywhere,) * 3,
        scratch_shapes=shapes,
        compiler_params=pltpu.CompilerParams(
            collective_id=0, has_side_effects=True, vmem_limit_bytes=64 * 1024 * 1024
        ),
    )(e_field, h_field, inverse_permittivity, monitor_layer, source_layer, residual_far, *consts)
    return pl.pallas_call(
        hand_out,
        out_shape=out_shape,
        in_specs=[anywhere] * 3,
        out_specs=(main,) * 3,
        scratch_shapes=[pltpu.VMEM(shape.shape, f32) for shape in out_shape] + [dma((3 + freqs + 3,))] * 2,
        compiler_params=pltpu.CompilerParams(vmem_limit_bytes=64 * 1024 * 1024),
    )(*results)


def solution(mesh):
    in_specs = (
        P("design", None, "gx", "gy"),
        P("design", None, "gx", "gy"),
        P("design", "gx", "gy"),
        P(("design", "gx"), "gy"),
        P(("design", "gx"), "gy"),
        P("design", None, None, "gx", "gy"),
    )
    out_specs = (
        P("design", None, "gx", "gy"),
        P("design", None, None, "gx", "gy"),
        P("design", None, "gx", "gy"),
    )
    gx, gy = mesh.shape["gx"], mesh.shape["gy"]

    def local(e_field, h_field, inverse_permittivity, monitor_layer, source_layer, residual_far):
        _, _, nx, ny = e_field.shape
        na, nb = residual_far.shape[3:]
        consts = [jnp.asarray(table) for table in tables(gx, gy, na, nb, nx, ny)]
        return per_device(consts, gx, gy, e_field, h_field, inverse_permittivity, monitor_layer,
                          source_layer, residual_far)

    return jax.shard_map(local, mesh=mesh, in_specs=in_specs, out_specs=out_specs, check_vma=False)
```
